1024 devices in a mesh: dp: 32 (over x, z_lo), tensor: 32 (over z_hi, y, core).
Axes of the slice: x: 4, y: 8, z: 16 (z_hi: 2, z_lo: 8; z = z_hi * 8 + z_lo), core: 2. Of those that a mesh axis runs over, the one named last changes fastest.
Arguments:
- x_source: bfloat16 [2048, 4096], P('dp', 'tensor'), may hold values from -6 to 6
- grad_out: bfloat16 [4096, 4096], P('dp'), may hold values from -6 to 6
- w_query: bfloat16 [4096, 4096], P(None, 'tensor'), may hold values from -0.09375 to 0.09375
- w_kv: bfloat16 [4096, 1024], P(None, 'tensor'), may hold values from -0.09375 to 0.09375
- w_out: bfloat16 [4096, 4096], P('tensor'), may hold values from -0.5 to 0.5
- lengths: int32 [32, 4], replicated, may hold values from 1 to 32, 64 in all within a row
- dest: int32 [32, 4], replicated, may hold values from 0 to 31, as said below
Outputs:
- grad_input: bfloat16 [4096, 4096], P('dp', 'tensor')
- grad_query: float32 [4096, 4096], P('dp', 'tensor')
- grad_kv: float32 [4096, 1024], P('dp', 'tensor')
- grad_wout: float32 [4096, 4096], P('tensor', 'dp')
The draws below stay inside these ranges and needn't reach their ends.
Inputs may be any that keep to these rules, and one draw needn't show every extreme that they name: `dest`: sequence j of every group g goes to group (g + c_j) mod 32 for 4 distinct shifts c_j, so each group receives exactly 4 sequences, at most one from any group. Each group's 4 lengths sum to 64, and the longest of all is 32.
All inputs are finite; a program needn't handle non-finite values.
Results may differ from the reference program's by a relative error of at most 0.034.
Values may be sent and summed in bfloat16 or wider, within the bound.
No kernel may reach another device: no remote copies, remote signals or barrier semaphores. Data moves between devices by JAX's collectives and lax.ppermute only.
A program may use at most 32 MiB of HBM per device.

```python
import math
import jax
import jax.numpy as jnp
import numpy as np
from jax import lax

D = 4096
HD = 128
SEQS = 4
MOST = 32
HEADS = 32
GROUP = 8
KVH = 4
TOK_DEV = 64
ROWS = 128
N_DP = 32


def draw_dest(key, part):
    key = jax.random.fold_in(key, 7)
    shuffled = jax.random.permutation(key, N_DP).astype(jnp.int32)
    ranks = jnp.argsort(shuffled).astype(jnp.int32)
    values = jnp.arange(N_DP, dtype=jnp.int32)
    forced = (values == 1) | (values == N_DP // 2)
    sort_key = jnp.where(forced, values - 2 * N_DP, ranks)
    chosen = jnp.argsort(sort_key)[:SEQS].astype(jnp.int32)
    order = jax.random.permutation(jax.random.fold_in(key, 11), SEQS)
    shifts = chosen[order]
    groups = jnp.arange(N_DP, dtype=jnp.int32)
    return (groups[:, None] + shifts[None, :]) % N_DP


def block_levels(own_key, dims, split, smallest, top_value):
    def one(position, shards_of):
        draws = jax.random.uniform(jax.random.fold_in(jax.random.fold_in(own_key, 6), position), (shards_of,), jnp.float32, smallest / len(split), top_value / len(split))
        return jnp.repeat(jnp.exp(draws), dims[position] // shards_of).reshape((-1,) + (1,) * (len(dims) - position - 1))

    loudness = one(*split[0])
    for cut in split[1:]:
        loudness = loudness * one(*cut)
    return loudness


def profile(amount, total, reach, slope):
    loads = [(1 << 20) // math.isqrt(rank ** slope) + 1 for rank in range(2, amount + 1)]
    spare, counts = total - reach - (amount - 1), [1] * (amount - 1)
    while spare > 0:
        free = [i for i in range(amount - 1) if counts[i] < reach]
        pool, budget = sum([loads[i] for i in free]), spare
        for i in free:
            addition = min(reach - counts[i], max(1, budget * loads[i] // pool), spare)
            counts[i] = counts[i] + addition
            spare = spare - addition
    return np.array([reach] + counts)


def uneven(key, amount, total, bound, slope):
    if amount == 2:
        one = jax.random.randint(key, (), max(1, total - bound), min(bound, total - 1) + 1)
        return jnp.stack([one, total - one])
    sizes = jnp.asarray(profile(amount, total, bound, slope), jnp.int32)
    twos = (amount - 1) // 2
    giver, sink = sizes[1:1 + 2 * twos:2], sizes[2:2 + 2 * twos:2]
    room = jnp.minimum(giver - 1, bound - sink)
    passed = jax.random.randint(jax.random.fold_in(key, 1), (twos,), 0, 1 << 20) % (room + 1)
    sizes = sizes.at[1:1 + 2 * twos:2].set(giver - passed).at[2:2 + 2 * twos:2].set(sink + passed)
    return sizes[jax.random.permutation(jax.random.fold_in(key, 2), amount)]


def bell_draw(own_key, shape, width, limit, cuts=(), kind=jnp.bfloat16):
    level = block_levels(own_key, shape, cuts, -0.22, 0.18) if cuts else 1.0
    array = jax.random.normal(own_key, shape, jnp.float32) * width * level
    return jnp.minimum(jnp.maximum(array, -limit), limit).astype(kind)


def setup_inputs(seed: int = 0) -> dict:
    seeds = jax.random.split(jax.random.key(seed), 8)
    return {
        "x_source": bell_draw(seeds[0], (N_DP * TOK_DEV, D), 1.0, 6.0, ((0, 32), (1, 32))),
        "grad_out": bell_draw(seeds[1], (N_DP * ROWS, D), 1.0, 6.0, ((0, 32),)),
        "w_query": bell_draw(seeds[2], (D, HEADS * HD), D ** -0.5, 0.09375, ((1, 32),)),
        "w_kv": bell_draw(seeds[3], (D, KVH * 2 * HD), D ** -0.5, 0.09375, ((1, 32),)),
        "w_out": bell_draw(seeds[4], (HEADS * HD, D), HD ** -0.5, 0.5, ((0, 32),)),
        "lengths": jax.vmap(lambda own: uneven(own, SEQS, TOK_DEV, MOST, 2))(jax.random.split(seeds[5], N_DP)).reshape((N_DP, SEQS)).astype(jnp.int32),
        "dest": draw_dest(jax.random.fold_in(seeds[7], 71), 0),
    }


def rope_tables(positions, head_dim):
    half_dim = head_dim // 2
    frequency = jnp.exp(jnp.arange(half_dim, dtype=jnp.float32) * (-2.0 * math.log(1000000.0) / head_dim))
    angles = positions.astype(jnp.float32)[..., None] * frequency
    cosine = jnp.cos(angles)
    sine = jnp.sin(angles)
    return (jnp.concatenate([cosine, cosine], -1), jnp.concatenate([sine, sine], -1))

def rotate(vectors, cosine, sine):
    half_dim = vectors.shape[-1] // 2
    leading = vectors[..., :half_dim]
    trailing = vectors[..., half_dim:]
    turned = jnp.concatenate([-trailing, leading], -1)
    return vectors * cosine + turned * sine

def arrangement(lengths, dest):
    groups = dest.shape[0]
    seq_total = dest.shape[1]
    starts = jnp.cumsum(lengths, axis=1).astype(jnp.int32) - lengths
    targets = jnp.arange(groups, dtype=jnp.int32)
    matches = (dest[None, :, :] == targets[:, None, None]).astype(jnp.int32)
    is_live = lax.optimization_barrier(jnp.sum(matches, axis=2))
    ranking = (1 - is_live) * groups + targets[None, :]
    senders = jnp.argsort(ranking, axis=1)[:, :seq_total].astype(jnp.int32)
    picked = jnp.take_along_axis(matches, senders[:, :, None], axis=1)
    seq_choice = lax.optimization_barrier(jnp.sum(picked * jnp.arange(seq_total, dtype=jnp.int32), axis=2)).astype(jnp.int32)
    return (senders, starts[senders, seq_choice], lengths[senders, seq_choice])

def attention(queries, key_rot, values, is_valid, grad_att, cosine, sine):
    inv_scale = 1.0 / math.sqrt(queries.shape[-1])
    longest = queries.shape[-2]
    position_in = jnp.arange(longest)
    scores = jnp.einsum('...qd,...kd->...qk', queries.astype(jnp.float32), key_rot.astype(jnp.float32)) * inv_scale
    allowed = (position_in[:, None] >= position_in[None, :]) & is_valid[..., None, :]
    scores = jnp.where(allowed, scores, -1e+30)
    highest = lax.optimization_barrier(jnp.max(scores, axis=-1, keepdims=True))
    weights = jnp.exp(scores - highest) * allowed.astype(jnp.float32)
    attn_probs = weights / lax.optimization_barrier(jnp.sum(weights, axis=-1, keepdims=True)) * is_valid[..., :, None].astype(jnp.float32)
    probs_low = attn_probs.astype(jnp.bfloat16)
    outputs = jnp.einsum('...qk,...kd->...qd', probs_low.astype(jnp.float32), values.astype(jnp.float32)).astype(jnp.bfloat16)
    grad_probs = jnp.einsum('...qd,...kd->...qk', grad_att.astype(jnp.float32), values.astype(jnp.float32))
    centre = lax.optimization_barrier(jnp.sum(attn_probs * grad_probs, axis=-1, keepdims=True))
    grad_scores = (attn_probs * (grad_probs - centre) * inv_scale).astype(jnp.bfloat16)
    grad_qrot = jnp.einsum('...qk,...kd->...qd', grad_scores.astype(jnp.float32), key_rot.astype(jnp.float32))
    grad_krot = jnp.einsum('...qk,...qd->...kd', grad_scores.astype(jnp.float32), queries.astype(jnp.float32))
    grad_values = jnp.einsum('...qk,...qd->...kd', probs_low.astype(jnp.float32), grad_att.astype(jnp.float32))
    grad_queries = rotate(grad_qrot, cosine, -sine).astype(jnp.bfloat16)
    grad_keys = rotate(grad_krot, cosine, -sine)
    return (outputs, grad_queries, grad_keys, grad_values)

def group_sum(partial_value):
    return lax.optimization_barrier(jnp.sum(lax.optimization_barrier(partial_value.astype(jnp.bfloat16)).astype(jnp.float32), axis=0))

def reference(x_source, grad_out, w_query, w_kv, w_out, lengths, dest):
    groups = dest.shape[0]
    seq_total = dest.shape[1]
    senders, seq_start, seq_len = arrangement(lengths, dest)
    position_in = jnp.arange(MOST, dtype=jnp.int32)
    is_valid = position_in[None, None, :] < seq_len[:, :, None]
    row_index = jnp.where(is_valid, senders[:, :, None] * TOK_DEV + seq_start[:, :, None] + position_in[None, None, :], 0).astype(jnp.int32)
    placed = jnp.where(is_valid[..., None], x_source[row_index], jnp.zeros((), x_source.dtype))
    cosine, sine = rope_tables(jnp.broadcast_to(position_in[None, None, :], (groups, seq_total, MOST)), HD)
    row_total = groups * seq_total * MOST
    flat_rows = placed.reshape(row_total, D)
    kv_proj = jnp.dot(flat_rows, w_kv, preferred_element_type=jnp.float32).astype(jnp.bfloat16)
    kv_proj = kv_proj.reshape(groups, seq_total, MOST, KVH, 2, HD)
    key_rot = rotate(kv_proj[..., 0, :].astype(jnp.float32), cosine[..., None, :], sine[..., None, :]).astype(jnp.bfloat16)
    values = kv_proj[..., 1, :]
    query_w = w_query.reshape(D, HEADS, HD).transpose(1, 0, 2)
    out_w = w_out.reshape(HEADS, HD, D)
    row_groups = flat_rows.reshape(groups, seq_total * MOST, D)
    grad_groups = grad_out.reshape(groups, seq_total * MOST, D)

    def one_head(packed):
        head_index, query_part, out_part = packed
        kv_index = head_index // GROUP
        queries = jnp.dot(flat_rows, query_part, preferred_element_type=jnp.float32).astype(jnp.bfloat16)
        queries = queries.reshape(groups, seq_total, MOST, HD)
        queries = rotate(queries.astype(jnp.float32), cosine, sine).astype(jnp.bfloat16)
        own_keys = jnp.take(key_rot, kv_index, axis=3)
        own_values = jnp.take(values, kv_index, axis=3)
        grad_att = lax.dot_general(grad_out, out_part, (((1,), (1,)), ((), ())), preferred_element_type=jnp.float32)
        grad_att = grad_att.astype(jnp.bfloat16).reshape(groups, seq_total, MOST, HD)
        outputs, grad_queries, grad_keys, grad_values = attention(queries, own_keys, own_values, is_valid, grad_att, cosine, sine)
        kv_term = jnp.stack([grad_keys, grad_values], axis=-2).astype(jnp.bfloat16)
        grad_wq = group_sum(jnp.einsum('grd,grh->gdh', row_groups.astype(jnp.float32), grad_queries.reshape(groups, -1, HD).astype(jnp.float32)))
        grad_wo = group_sum(jnp.einsum('grh,grd->ghd', outputs.reshape(groups, -1, HD).astype(jnp.float32), grad_groups.astype(jnp.float32)))
        return (grad_queries, kv_term, grad_wq, grad_wo)
    head_ids = jnp.arange(HEADS, dtype=jnp.int32)
    grad_queries, kv_terms, grad_wq, grad_wo = lax.map(one_head, (head_ids, query_w, out_w))
    kv_terms = lax.optimization_barrier(kv_terms).astype(jnp.float32)
    kv_sum = lax.optimization_barrier(jnp.sum(kv_terms.reshape((KVH, GROUP) + kv_terms.shape[1:]), axis=1))
    kv_grad = kv_sum.transpose(1, 2, 3, 0, 4, 5).astype(jnp.bfloat16).reshape(row_total, KVH * 2 * HD)
    col_width = KVH * 2 * HD // HEADS
    kv_blocks = kv_grad.reshape(row_total, HEADS, col_width).transpose(1, 0, 2)
    wkv_blocks = w_kv.reshape(D, HEADS, col_width).transpose(1, 0, 2)

    def add_block(total, packed):
        query_grad, query_part, kv_part, wkv_part = packed
        partial_value = lax.dot_general(query_grad, query_part, (((1,), (1,)), ((), ())), preferred_element_type=jnp.float32)
        partial_value = partial_value + lax.dot_general(kv_part, wkv_part, (((1,), (1,)), ((), ())), preferred_element_type=jnp.float32)
        return (total + lax.optimization_barrier(partial_value.astype(jnp.bfloat16)).astype(jnp.float32), None)
    total, _ = lax.scan(add_block, jnp.zeros((row_total, D), jnp.float32), (grad_queries.reshape(HEADS, row_total, HD), query_w, kv_blocks, wkv_blocks))
    grad_input = total.astype(jnp.bfloat16)
    grad_query = grad_wq.transpose(1, 0, 2).reshape(D, HEADS * HD)
    grad_kv = group_sum(jnp.einsum('grd,grc->gdc', row_groups.astype(jnp.float32), kv_grad.reshape(groups, -1, KVH * 2 * HD).astype(jnp.float32)))
    grad_wout = grad_wo.reshape(HEADS * HD, D)
    return (grad_input, grad_query, grad_kv, grad_wout)
```

```python
import math

import jax
import jax.numpy as jnp
import numpy as np
from jax import lax
from jax.experimental import pallas as pl
from jax.experimental.pallas import tpu as pltpu
from jax.sharding import Mesh
from jax.sharding import PartitionSpec as P

DP = ("x", "zl")
YY = ("yh", "yl")
TP = ("zh", "yh", "yl", "c")
PEERS = ("yl", "c")
F32 = jnp.float32
BF16 = jnp.bfloat16


def dot(left, right, dims):
    return lax.dot_general(left, right, (dims, ((), ())), preferred_element_type=F32)


def tables(longest, seq_total, head_dim):
    frequency = np.exp(
        np.arange(head_dim // 2, dtype=np.float32) * np.float32(-2.0 * math.log(1000000.0) / head_dim)
    ).astype(np.float32)
    angles = (np.arange(longest, dtype=np.float32)[:, None] * frequency).astype(np.float32)
    cosine, sine = np.cos(angles), np.sin(angles)
    cosine = np.tile(np.concatenate([cosine, cosine], -1), (seq_total, 1)).astype(np.float32)
    signed = np.tile(np.concatenate([-sine, sine], -1), (seq_total, 1)).astype(np.float32)
    return cosine, signed


def block_at(zh, y, c):
    return zh * 16 + y * 2 + c


def project_kernel(x_ref, wq_ref, wkv_ref, q_ref, kv_ref):
    rows = x_ref.shape[3]
    q = jnp.zeros((rows, 128), F32)
    kv = jnp.zeros((32, rows), F32)
    for c in range(2):
        for y in range(8):
            for zh in range(2):
                xb = x_ref[c, y, zh]
                cut = pl.ds(block_at(zh, y, c) * 128, 128)
                q = q + dot(xb, wq_ref[cut, :], ((1,), (0,)))
                kv = kv + dot(wkv_ref[cut, :], xb, ((0,), (1,)))
    q_ref[...] = q.astype(BF16)
    kv_ref[...] = kv.astype(BF16)


def attention_kernel(longest, len_ref, q_ref, kv_ref, ga_ref, cos_ref, sin_ref, cost_ref, sint_ref,
                     o_ref, gq_ref, kvg_ref):
    rows, hd = q_ref.shape
    inv_scale = 1.0 / math.sqrt(hd)

    def turn(v):
        return jnp.concatenate([v[:, hd // 2:], v[:, : hd // 2]], 1)

    def turn_t(v):
        return jnp.concatenate([v[hd // 2:], v[: hd // 2]], 0)

    cosine, sine, cosine_t, sine_t = cos_ref[...], sin_ref[...], cost_ref[...], sint_ref[...]
    q = q_ref[...].astype(F32)
    q = (q * cosine + turn(q) * sine).astype(BF16)
    k = kv_ref[:hd, :].astype(F32)
    k = (k * cosine_t + turn_t(k) * sine_t).astype(BF16)
    v = kv_ref[hd:, :]
    ga = ga_ref[...]
    qi = lax.broadcasted_iota(jnp.int32, (rows, rows), 0)
    ki = lax.broadcasted_iota(jnp.int32, (rows, rows), 1)
    ends = jnp.zeros((rows, rows), jnp.int32)
    starts = jnp.zeros((rows, rows), jnp.int32)
    for slot in range(rows // longest):
        here = (qi >= slot * longest) & (qi < (slot + 1) * longest)
        starts = jnp.where(here, slot * longest, starts)
        ends = jnp.where(here, slot * longest + len_ref[slot], ends)
    allowed = (ki >= starts) & (ki <= qi) & (ki < ends)
    scores = jnp.where(allowed, dot(q, k, ((1,), (0,))) * inv_scale, -1e30)
    highest = jnp.max(scores, axis=1, keepdims=True)
    weights = jnp.where(allowed, jnp.exp(scores - highest), 0.0)
    probs = weights / jnp.sum(weights, axis=1, keepdims=True)
    probs = jnp.where(qi < ends, probs, 0.0)
    low = probs.astype(BF16)
    o_ref[...] = dot(low, v, ((1,), (1,))).astype(BF16)
    gp = dot(ga, v, ((1,), (0,)))
    centre = jnp.sum(probs * gp, axis=1, keepdims=True)
    gs = (probs * (gp - centre) * inv_scale).astype(BF16)
    gq = dot(gs, k, ((1,), (1,)))
    gq_ref[...] = (gq * cosine - turn(gq) * sine).astype(BF16)
    gk = dot(q, gs, ((0,), (0,)))
    kvg_ref[:hd, :] = (gk * cosine_t - turn_t(gk) * sine_t).astype(BF16)
    kvg_ref[hd:, :] = dot(ga, low, ((0,), (0,))).astype(BF16)


def product_kernel(own_ref, x_ref, go_ref, wq_ref, wkv_ref, o_ref, gq_ref, kvg_ref, gw_ref, mine_ref, other_ref):
    gq = gq_ref[...]
    out = o_ref[...]
    kvg = kvg_ref[...]
    for zh in range(2):
        for y in range(8):
            for c in range(2):
                block = block_at(zh, y, c)
                cut = pl.ds(block * 128, 128)
                xb = x_ref[c, y, zh]
                to = (block // 8, block % 8)
                gw_ref[to[0], to[1], 0:128, :] = dot(xb, gq, ((0,), (0,))).astype(BF16)
                gw_ref[to[0], to[1], 128:256, :] = dot(out, go_ref[:, cut], ((0,), (0,))).astype(BF16)
                gw_ref[to[0], to[1], 256:288, :] = dot(kvg, xb, ((1,), (0,))).astype(BF16)
    own = own_ref[0]
    for c in range(2):
        for y in range(8):
            for zh in range(2):
                cut = pl.ds(block_at(zh, y, c) * 128, 128)
                part = dot(gq, wq_ref[cut, :], ((1,), (1,))) + dot(kvg, wkv_ref[cut, :], ((0,), (1,)))
                part = part.astype(BF16)

                @pl.when(own == c)
                def _():
                    mine_ref[y, zh] = part

                @pl.when(own != c)
                def _():
                    other_ref[y, zh] = part


def body(x_source, grad_out, w_query, w_kv, w_out, lengths, dest):
    groups, seq_total = dest.shape
    rows = grad_out.shape[0]
    longest = rows // seq_total
    group = lax.axis_index(DP)
    own_zh = lax.axis_index("zh")
    own_c = lax.axis_index("c")
    swap = [(0, 1), (1, 0)]
    vmem = pl.BlockSpec(memory_space=pltpu.VMEM)
    smem = pl.BlockSpec(memory_space=pltpu.SMEM)
    params = pltpu.CompilerParams(vmem_limit_bytes=40 * 1024 * 1024)
    shape = jax.ShapeDtypeStruct

    shifts = dest[0]
    own_len = lax.dynamic_index_in_dim(lengths, group, 0, keepdims=False)
    own_start = jnp.cumsum(own_len) - own_len
    own_dest = (group + shifts) % groups
    slot = jnp.arange(groups, dtype=jnp.int32)[:, None, None, None]
    place = jnp.arange(longest, dtype=jnp.int32)[None, :, None, None]
    token = jnp.arange(x_source.shape[0], dtype=jnp.int32)[None, None, :, None]
    chosen = (slot == own_dest) & (place < own_len) & (token == own_start + place)
    chosen = jnp.any(chosen, axis=3).astype(BF16).reshape(groups * longest, -1)
    outgoing = dot(chosen, x_source, ((1,), (0,))).astype(BF16).reshape(groups, longest, -1)
    received = lax.all_to_all(outgoing, DP, 0, 0, tiled=True)

    sender = (group - shifts) % groups
    length = jnp.sum(
        jnp.where(jnp.arange(groups)[:, None] == sender[None, :], lengths, 0), axis=0
    )
    rank = jnp.sum((sender[None, :] < sender[:, None]).astype(jnp.int32), axis=1)
    pick = rank[None, :] == jnp.arange(seq_total)[:, None]
    my_senders = jnp.sum(jnp.where(pick, sender[None, :], 0), axis=1)
    my_len = jnp.sum(jnp.where(pick, length[None, :], 0), axis=1)
    xs = received[my_senders].reshape(rows, -1)

    xo = lax.ppermute(xs, "zh", swap)
    pair = jnp.where(own_zh == 0, jnp.stack([xs, xo]), jnp.stack([xo, xs]))
    wide = lax.all_to_all(jnp.broadcast_to(pair[None], (8,) + pair.shape), YY, 0, 0, tiled=True)
    xall = lax.all_gather(wide, "c", axis=0)

    q, kv = pl.pallas_call(
        project_kernel,
        out_shape=(shape((rows, 128), BF16), shape((32, rows), BF16)),
        in_specs=[vmem] * 3,
        out_specs=(vmem, vmem),
        compiler_params=params,
    )(xall, w_query, w_kv)
    kv = lax.all_to_all(jnp.broadcast_to(kv[None], (8,) + kv.shape), PEERS, 0, 0, tiled=True)
    kv = kv.reshape(256, rows)
    grad_att = dot(grad_out, w_out, ((1,), (1,))).astype(BF16)
    cosine, sine = tables(longest, seq_total, 128)
    out, gq, kvt = pl.pallas_call(
        lambda *refs: attention_kernel(longest, *refs),
        out_shape=(shape((rows, 128), BF16), shape((rows, 128), BF16), shape((256, rows), BF16)),
        in_specs=[smem] + [vmem] * 7,
        out_specs=(vmem,) * 3,
        compiler_params=params,
    )(my_len, q, kv, grad_att, cosine, sine, cosine.T.copy(), sine.T.copy())
    kvt = lax.all_to_all(kvt.reshape(8, 32, rows), PEERS, 0, 0, tiled=True)
    kvg = jnp.sum(kvt.astype(F32), axis=0).astype(BF16)

    gw, mine, other = pl.pallas_call(
        product_kernel,
        out_shape=(shape((4, 8, 288, 128), BF16), shape((8, 2, rows, 128), BF16), shape((8, 2, rows, 128), BF16)),
        in_specs=[smem] + [vmem] * 7,
        out_specs=(vmem,) * 3,
        compiler_params=params,
    )(own_c[None].astype(jnp.int32), xall, grad_out, w_query, w_kv, out, gq, kvg)

    theirs = lax.ppermute(other, "c", swap)
    half = (mine.astype(F32) + theirs.astype(F32)).astype(BF16)
    half = lax.all_to_all(half, YY, 0, 0, tiled=True)
    half = jnp.sum(half.astype(F32), axis=0)
    keep = jnp.where(own_zh == 0, half[0], half[1])
    send = jnp.where(own_zh == 0, half[1], half[0]).astype(BF16)
    grad_input = (keep + lax.ppermute(send, "zh", swap).astype(F32)).astype(BF16)

    gw = lax.all_to_all(gw, "x", 0, 0, tiled=True)
    gw = jnp.sum(gw.astype(F32), axis=0).astype(BF16)
    gw = lax.all_to_all(gw, "zl", 0, 0, tiled=True)
    gw = jnp.sum(gw.astype(F32), axis=0)
    return grad_input, gw[:128], gw[256:].T, gw[128:256]


def solution(mesh):
    fine = Mesh(mesh.devices.reshape(4, 8, 2, 2, 4, 2), ("x", "zl", "zh", "yh", "yl", "c"))
    placed = (P(DP, TP), P(DP, None), P(None, TP), P(None, TP), P(TP, None), P(), P())
    return jax.shard_map(
        body,
        mesh=fine,
        in_specs=placed,
        out_specs=(P(DP, TP), P(DP, TP), P(DP, TP), P(TP, DP)),
        check_vma=False,
    )
```

```python
import math

import jax
import jax.numpy as jnp
import numpy as np
from jax import lax
from jax.experimental import pallas as pl
from jax.experimental.pallas import tpu as pltpu
from jax.sharding import Mesh
from jax.sharding import PartitionSpec as P

AXES = ("x", "zb", "za", "zh", "yh", "yl", "c")
SIZES = (4, 2, 4, 2, 2, 4, 2)
DP = ("x", "zb", "za")
YY = ("yh", "yl")
TP = ("zh", "yh", "yl", "c")
PEERS = ("yl", "c")
F32 = jnp.float32
BF16 = jnp.bfloat16
SWAP = [(0, 1), (1, 0)]
G, OX, OC, OYL = 0, 1, 2, 3


def dot(left, right, dims):
    return lax.dot_general(left, right, (dims, ((), ())), preferred_element_type=F32)


def tables(longest, seq_total, head_dim):
    frequency = np.exp(
        np.arange(head_dim // 2, dtype=np.float32) * np.float32(-2.0 * math.log(1000000.0) / head_dim)
    ).astype(np.float32)
    angles = (np.arange(longest, dtype=np.float32)[:, None] * frequency).astype(np.float32)
    cosine, sine = np.cos(angles), np.sin(angles)
    cosine = np.tile(np.concatenate([cosine, cosine], -1), (seq_total, 1)).astype(np.float32)
    signed = np.tile(np.concatenate([-sine, sine], -1), (seq_total, 1)).astype(np.float32)
    return cosine, signed


def aligned(index, size):
    return pl.ds(pl.multiple_of(index * size, size), size)


def incoming(ids_ref, dest_ref):
    groups, seq_total = dest_ref.shape
    senders = [lax.rem(ids_ref[G] + groups - dest_ref[0, j], groups) for j in range(seq_total)]
    ranks = []
    for j in range(seq_total):
        rank = jnp.int32(0)
        for i in range(seq_total):
            rank = rank + (senders[i] < senders[j]).astype(jnp.int32)
        ranks.append(rank)
    return senders, ranks


def outgoing_kernel(ids_ref, len_ref, dest_ref, x_ref, out_ref):
    groups, seq_total = dest_ref.shape
    longest = out_ref.shape[1]
    tokens = x_ref.shape[0]
    group = ids_ref[G]
    out_ref[...] = jnp.zeros_like(out_ref)
    place = lax.broadcasted_iota(jnp.int32, (longest, tokens), 0)
    token = lax.broadcasted_iota(jnp.int32, (longest, tokens), 1)
    start = jnp.int32(0)
    for j in range(seq_total):
        size = len_ref[group, j]
        chosen = jnp.where((token == place + start) & (place < size), 1.0, 0.0).astype(BF16)
        to = lax.rem(group + dest_ref[0, j], groups)
        out_ref[to] = dot(chosen, x_ref[...], ((1,), (0,))).astype(BF16)
        start = start + size


def incoming_kernel(ids_ref, dest_ref, x_ref, *refs):
    out_ref = refs[-1]
    longest = x_ref.shape[1]
    senders, ranks = incoming(ids_ref, dest_ref)
    for sender, rank in zip(senders, ranks):
        rows = x_ref[sender]
        for i in range(out_ref.shape[0]):
            out_ref[i, aligned(rank, longest), :] = rows


def head_kernel(ids_ref, *refs):
    out_ref = refs[-1]
    for rel in range(4):
        for flip in range(2):
            peer = (ids_ref[OYL] ^ rel) * 2 + (ids_ref[OC] ^ flip)
            source = refs[rel] if flip == 0 else refs[4].at[rel]
            out_ref[aligned(peer, 32), :] = source[...]


def attention_kernel(longest, ids_ref, len_ref, dest_ref, xm_ref, xt_ref, wq_ref, wh_ref, ga_ref,
                     cos_ref, sin_ref, cost_ref, sint_ref, o_ref, gq_ref, kvg_ref, gap_ref):
    rows, hd = ga_ref.shape
    inv_scale = 1.0 / math.sqrt(hd)

    def turn(v):
        return jnp.concatenate([v[:, hd // 2:], v[:, : hd // 2]], 1)

    def turn_t(v):
        return jnp.concatenate([v[hd // 2:], v[: hd // 2]], 0)

    q = jnp.zeros((rows, hd), F32)
    kv = jnp.zeros((2 * hd, rows), F32)
    for x_ref, c in ((xm_ref, ids_ref[OC]), (xt_ref, 1 - ids_ref[OC])):
        for i in range(16):
            cut = aligned(i * 2 + c, 128)
            q = q + dot(x_ref[i], wq_ref[cut, :], ((1,), (0,)))
            kv = kv + dot(wh_ref[:, cut], x_ref[i], ((1,), (1,)))
    cosine, sine, cosine_t, sine_t = cos_ref[...], sin_ref[...], cost_ref[...], sint_ref[...]
    q = q.astype(BF16).astype(F32)
    q = (q * cosine + turn(q) * sine).astype(BF16)
    kv = kv.astype(BF16)
    k = kv[:hd].astype(F32)
    k = (k * cosine_t + turn_t(k) * sine_t).astype(BF16)
    v = kv[hd:]
    ga = ga_ref[...]
    qi = lax.broadcasted_iota(jnp.int32, (rows, rows), 0)
    ki = lax.broadcasted_iota(jnp.int32, (rows, rows), 1)
    ends = jnp.zeros((rows, rows), jnp.int32)
    starts = jnp.zeros((rows, rows), jnp.int32)
    senders, ranks = incoming(ids_ref, dest_ref)
    for j in range(rows // longest):
        first = ranks[j] * longest
        here = (qi >= first) & (qi < first + longest)
        starts = jnp.where(here, first, starts)
        ends = jnp.where(here, first + len_ref[senders[j], j], ends)
    allowed = (ki >= starts) & (ki <= qi) & (ki < ends)
    scores = jnp.where(allowed, dot(q, k, ((1,), (0,))) * inv_scale, -1e30)
    highest = jnp.max(scores, axis=1, keepdims=True)
    weights = jnp.where(allowed, jnp.exp(scores - highest), 0.0)
    probs = weights / jnp.sum(weights, axis=1, keepdims=True)
    probs = jnp.where(qi < ends, probs, 0.0)
    low = probs.astype(BF16)
    o_ref[...] = dot(low, v, ((1,), (1,))).astype(BF16)
    gp = dot(ga, v, ((1,), (0,)))
    centre = jnp.sum(probs * gp, axis=1, keepdims=True)
    gs = (probs * (gp - centre) * inv_scale).astype(BF16)
    gq = dot(gs, k, ((1,), (1,)))
    gq_ref[...] = (gq * cosine - turn(gq) * sine).astype(BF16)
    gk = dot(q, gs, ((0,), (0,)))
    gk = (gk * cosine_t - turn_t(gk) * sine_t).astype(BF16)
    gv = dot(ga, low, ((0,), (0,))).astype(BF16)
    kvg_ref[:hd, :] = gk
    kvg_ref[hd:, :] = gv
    gap_ref[:, :hd] = gk.astype(F32).T.astype(BF16)
    gap_ref[:, hd:] = gv.astype(F32).T.astype(BF16)


def input_kernel(ids_ref, wq_ref, wh_ref, gq_ref, kvt_ref, mine_ref, other_ref):
    gq, kvt = gq_ref[...], kvt_ref[...]
    for out_ref, c in ((other_ref, 1 - ids_ref[OC]), (mine_ref, ids_ref[OC])):
        for y in range(8):
            for zh in range(2):
                cut = aligned(zh * 16 + y * 2 + c, 128)
                part = dot(gq, wq_ref[cut, :], ((1,), (1,))) + dot(kvt, wh_ref[:, cut], ((1,), (0,)))
                out_ref[y, zh] = part.astype(BF16)


def row_of(yl, c):
    return ((yl & 1) * 2 + c) * 2 + (yl >> 1)


def weight_kernel(ids_ref, xm_ref, xt_ref, go_ref, o_ref, gq_ref, *out_refs):
    gq, out = gq_ref[...], o_ref[...]
    for s in (1, 2, 3, 0):
        x = (ids_ref[OX] + s) & 3
        for x_ref, c in ((xm_ref, ids_ref[OC]), (xt_ref, 1 - ids_ref[OC])):
            for yl in range(4):
                row = row_of(yl, c)
                out_refs[s][row, 0:128, :] = dot(x_ref[x * 4 + yl], gq, ((0,), (0,))).astype(BF16)
                cut = aligned(x * 8 + yl * 2 + c, 128)
                out_refs[s][row, 128:256, :] = dot(out, go_ref[:, cut], ((0,), (0,))).astype(BF16)


def half_kernel(mine_ref, theirs_ref, after_ref, out_ref):
    out_ref[...] = (mine_ref[...].astype(F32) + theirs_ref[...].astype(F32)).astype(BF16)


def kv_kernel(ids_ref, xm_ref, xt_ref, kvt_ref, *out_refs):
    kvg = jnp.sum(kvt_ref[...].astype(F32), axis=0).astype(BF16)
    for s in (1, 2, 3, 0):
        x = (ids_ref[OX] + s) & 3
        for x_ref, c in ((xm_ref, ids_ref[OC]), (xt_ref, 1 - ids_ref[OC])):
            for yl in range(4):
                part = dot(kvg, x_ref[x * 4 + yl], ((1,), (0,)))
                out_refs[s][row_of(yl, c)] = part.astype(BF16)


def sum_kernel(*refs):
    out_ref = refs[-1]
    out_ref[:, 0:256, :] = sum(ref[...].astype(F32) for ref in refs[:4]).astype(BF16)
    out_ref[:, 256:288, :] = sum(ref[...].astype(F32) for ref in refs[4:8]).astype(BF16)


def body(x_source, grad_out, w_query, w_kv, w_out, lengths, dest):
    groups, seq_total = dest.shape
    rows = grad_out.shape[0]
    longest = rows // seq_total
    vmem = pl.BlockSpec(memory_space=pltpu.VMEM)
    smem = pl.BlockSpec(memory_space=pltpu.SMEM)
    anyw = pl.BlockSpec(memory_space=pl.ANY)
    params = pltpu.CompilerParams(vmem_limit_bytes=32 * 1024 * 1024)
    shape = jax.ShapeDtypeStruct
    own_x, own_c, own_yl = lax.axis_index("x"), lax.axis_index("c"), lax.axis_index("yl")
    own_zh, own_zb = lax.axis_index("zh"), lax.axis_index("zb")
    ids = jnp.stack([lax.axis_index(DP), own_x, own_c, own_yl]).astype(jnp.int32)

    def call(kernel, ins, outs, out_shape, **extra):
        return pl.pallas_call(
            kernel, out_shape=out_shape, in_specs=ins, out_specs=outs, compiler_params=params, **extra
        )

    outgoing = call(outgoing_kernel, [smem] * 3 + [vmem], vmem, shape((groups, longest, 128), BF16))(
        ids, lengths, dest, x_source
    )
    received = lax.all_to_all(outgoing, DP, 0, 0, tiled=True)
    w_own = w_kv.T
    w_parts = [w_own] + [lax.ppermute(w_own, "yl", [(i, i ^ s) for i in range(4)]) for s in (1, 2, 3)]
    w_there = lax.ppermute(jnp.stack(w_parts), "c", SWAP)
    w_head = call(head_kernel, [smem] + [vmem] * 5, vmem, shape((256, w_kv.shape[0]), BF16))(
        ids, *w_parts, w_there
    )
    grad_att = dot(grad_out, w_out, ((1,), (1,))).astype(BF16)

    spread = call(incoming_kernel, [smem] * 2 + [vmem] + [anyw] * 3, vmem, shape((16, rows, 128), BF16))(
        ids, dest, received, *w_parts[1:]
    )
    x_mine = lax.all_to_all(spread, ("zh",) + YY, 0, 0, tiled=True)
    x_there = lax.ppermute(x_mine, "c", SWAP)

    cosine, sine = tables(longest, seq_total, 128)
    out, gq, kv_term, kv_turned = call(
        lambda *refs: attention_kernel(longest, *refs),
        [smem] * 3 + [vmem] * 9,
        (vmem,) * 4,
        (shape((rows, 128), BF16), shape((rows, 128), BF16), shape((256, rows), BF16), shape((rows, 256), BF16)),
    )(ids, lengths, dest, x_mine, x_there, w_query, w_head, grad_att, cosine, sine, cosine.T.copy(), sine.T.copy())
    kv_terms = lax.all_to_all(kv_term.reshape(8, 32, rows), PEERS, 0, 0, tiled=True)

    half = shape((8, 2, rows, 128), BF16)
    mine, other = call(input_kernel, [smem] + [vmem] * 4, (vmem,) * 2, (half, half))(
        ids, w_query, w_head, gq, kv_turned
    )
    theirs = lax.ppermute(other, "c", SWAP)
    gw = call(weight_kernel, [smem] + [vmem] * 5, (vmem,) * 4, (shape((8, 256, 128), BF16),) * 4)(
        ids, x_mine, x_there, grad_out, out, gq
    )
    part = call(half_kernel, [vmem] * 2 + [anyw], vmem, half)(mine, theirs, gw[0])
    gkv = call(kv_kernel, [smem] + [vmem] * 3, (vmem,) * 4, (shape((8, 32, 128), BF16),) * 4)(
        ids, x_mine, x_there, kv_terms
    )
    part = lax.all_to_all(part, YY, 0, 0, tiled=True)
    part = jnp.sum(part.astype(F32), axis=0)
    keep = jnp.where(own_zh == 0, part[0], part[1])
    send = jnp.where(own_zh == 0, part[1], part[0]).astype(BF16)
    grad_input = (keep + lax.ppermute(send, "zh", SWAP).astype(F32)).astype(BF16)

    around = [[(i, (i + s) % 4) for i in range(4)] for s in range(4)]
    gw = [gw[0]] + [lax.ppermute(gw[s], "x", around[s]) for s in (1, 2, 3)]
    gkv = [gkv[0]] + [lax.ppermute(gkv[s], "x", around[s]) for s in (1, 2, 3)]
    total = call(sum_kernel, [vmem] * 8, vmem, shape((8, 288, 128), BF16))(*gw, *gkv)
    total = lax.all_to_all(total.reshape(4, 576, 128), "za", 0, 0, tiled=True)
    total = jnp.sum(total.astype(F32), axis=0).reshape(2, 288, 128)
    keep = jnp.where(own_zb == 0, total[0], total[1])
    send = jnp.where(own_zb == 0, total[1], total[0]).astype(BF16)
    total = keep + lax.ppermute(send, "zb", SWAP).astype(F32)
    return grad_input, total[:128], total[256:].T, total[128:256]


def solution(mesh):
    fine = Mesh(mesh.devices.reshape(SIZES), AXES)
    placed = (P(DP, TP), P(DP, None), P(None, TP), P(None, TP), P(TP, None), P(), P())
    return jax.shard_map(
        body,
        mesh=fine,
        in_specs=placed,
        out_specs=(P(DP, TP), P(DP, TP), P(DP, TP), P(TP, DP)),
        check_vma=False,
    )
```

```python
import math

import jax
import jax.numpy as jnp
import numpy as np
from jax import lax
from jax.experimental import pallas as pl
from jax.experimental.pallas import tpu as pltpu
from jax.sharding import Mesh
from jax.sharding import PartitionSpec as P

AXES = ("x", "zb", "za", "zh", "yh", "yl", "c")
SIZES = (4, 2, 4, 2, 2, 4, 2)
DP = ("x", "zb", "za")
YY = ("yh", "yl")
TP = ("zh", "yh", "yl", "c")
PEERS = ("yl", "c")
F32 = jnp.float32
BF16 = jnp.bfloat16
SWAP = [(0, 1), (1, 0)]
G, OX, OC, OYL, OZH = 0, 1, 2, 3, 4


def dot(left, right, dims):
    return lax.dot_general(left, right, (dims, ((), ())), preferred_element_type=F32)


def tables(longest, seq_total, head_dim):
    frequency = np.exp(
        np.arange(head_dim // 2, dtype=np.float32) * np.float32(-2.0 * math.log(1000000.0) / head_dim)
    ).astype(np.float32)
    angles = (np.arange(longest, dtype=np.float32)[:, None] * frequency).astype(np.float32)
    cosine, sine = np.cos(angles), np.sin(angles)
    cosine = np.tile(np.concatenate([cosine, cosine], -1), (seq_total, 1)).astype(np.float32)
    signed = np.tile(np.concatenate([-sine, sine], -1), (seq_total, 1)).astype(np.float32)
    return cosine, signed


def aligned(index, size):
    return pl.ds(pl.multiple_of(index * size, size), size)


def incoming(ids_ref, dest_ref):
    groups, seq_total = dest_ref.shape
    senders = [lax.rem(ids_ref[G] + groups - dest_ref[0, j], groups) for j in range(seq_total)]
    ranks = []
    for j in range(seq_total):
        rank = jnp.int32(0)
        for i in range(seq_total):
            rank = rank + (senders[i] < senders[j]).astype(jnp.int32)
        ranks.append(rank)
    return senders, ranks


def outgoing_kernel(ids_ref, len_ref, dest_ref, x_ref, out_ref):
    groups, seq_total = dest_ref.shape
    longest = out_ref.shape[1]
    tokens = x_ref.shape[0]
    group = ids_ref[G]
    out_ref[...] = jnp.zeros_like(out_ref)
    place = lax.broadcasted_iota(jnp.int32, (longest, tokens), 0)
    token = lax.broadcasted_iota(jnp.int32, (longest, tokens), 1)
    start = jnp.int32(0)
    for j in range(seq_total):
        size = len_ref[group, j]
        chosen = jnp.where((token == place + start) & (place < size), 1.0, 0.0).astype(BF16)
        to = lax.rem(group + dest_ref[0, j], groups)
        out_ref[to] = dot(chosen, x_ref[...], ((1,), (0,))).astype(BF16)
        start = start + size


def incoming_kernel(ids_ref, dest_ref, x_ref, *refs):
    own_ref, out_ref = refs[-2:]
    longest = x_ref.shape[1]
    senders, ranks = incoming(ids_ref, dest_ref)
    for sender, rank in zip(senders, ranks):
        rows = x_ref[sender]
        own_ref[aligned(rank, longest), :] = rows
        for i in range(out_ref.shape[0]):
            out_ref[i, aligned(rank, longest), :] = rows


def stack_kernel(*refs):
    out_ref = refs[-1]
    for rel in range(4):
        out_ref[rel] = refs[rel][...]


def head_kernel(ids_ref, here_ref, there_ref, out_ref):
    for rel in range(4):
        for flip, source in enumerate((here_ref, there_ref)):
            peer = (ids_ref[OYL] ^ rel) * 2 + (ids_ref[OC] ^ flip)
            out_ref[aligned(peer, 32), :] = source[rel]


def attention_kernel(longest, ids_ref, len_ref, dest_ref, x0_ref, x1_ref, x2_ref, x3_ref, wq_ref, wh_ref, ga_ref,
                     cos_ref, sin_ref, cost_ref, sint_ref, o_ref, gq_ref, kvg_ref, gap_ref, x_ref):
    rows, hd = ga_ref.shape
    inv_scale = 1.0 / math.sqrt(hd)

    def turn(v):
        return jnp.concatenate([v[:, hd // 2:], v[:, : hd // 2]], 1)

    def turn_t(v):
        return jnp.concatenate([v[hd // 2:], v[: hd // 2]], 0)

    q = jnp.zeros((rows, hd), F32)
    kv = jnp.zeros((2 * hd, rows), F32)
    zh, c = ids_ref[OZH], ids_ref[OC]
    for part_ref, z, core in ((x0_ref, zh, c), (x1_ref, 1 - zh, c), (x2_ref, zh, 1 - c), (x3_ref, 1 - zh, 1 - c)):
        for y in range(8):
            block = z * 16 + y * 2 + core
            cut = aligned(block, 128)
            xb = part_ref[y]
            x_ref[block] = xb
            q = q + dot(xb, wq_ref[cut, :], ((1,), (0,)))
            kv = kv + dot(wh_ref[:, cut], xb, ((1,), (1,)))
    cosine, sine, cosine_t, sine_t = cos_ref[...], sin_ref[...], cost_ref[...], sint_ref[...]
    q = q.astype(BF16).astype(F32)
    q = (q * cosine + turn(q) * sine).astype(BF16)
    kv = kv.astype(BF16)
    k = kv[:hd].astype(F32)
    k = (k * cosine_t + turn_t(k) * sine_t).astype(BF16)
    v = kv[hd:]
    ga = ga_ref[...]
    qi = lax.broadcasted_iota(jnp.int32, (rows, rows), 0)
    ki = lax.broadcasted_iota(jnp.int32, (rows, rows), 1)
    ends = jnp.zeros((rows, rows), jnp.int32)
    starts = jnp.zeros((rows, rows), jnp.int32)
    senders, ranks = incoming(ids_ref, dest_ref)
    for j in range(rows // longest):
        first = ranks[j] * longest
        here = (qi >= first) & (qi < first + longest)
        starts = jnp.where(here, first, starts)
        ends = jnp.where(here, first + len_ref[senders[j], j], ends)
    allowed = (ki >= starts) & (ki <= qi) & (ki < ends)
    scores = jnp.where(allowed, dot(q, k, ((1,), (0,))) * inv_scale, -1e30)
    highest = jnp.max(scores, axis=1, keepdims=True)
    weights = jnp.where(allowed, jnp.exp(scores - highest), 0.0)
    probs = weights / jnp.sum(weights, axis=1, keepdims=True)
    probs = jnp.where(qi < ends, probs, 0.0)
    low = probs.astype(BF16)
    o_ref[...] = dot(low, v, ((1,), (1,))).astype(BF16)
    gp = dot(ga, v, ((1,), (0,)))
    centre = jnp.sum(probs * gp, axis=1, keepdims=True)
    gs = (probs * (gp - centre) * inv_scale).astype(BF16)
    gq = dot(gs, k, ((1,), (1,)))
    gq_ref[...] = (gq * cosine - turn(gq) * sine).astype(BF16)
    gk = dot(q, gs, ((0,), (0,)))
    gk = (gk * cosine_t - turn_t(gk) * sine_t).astype(BF16)
    gv = dot(ga, low, ((0,), (0,))).astype(BF16)
    kvg_ref[:hd, :] = gk
    kvg_ref[hd:, :] = gv
    gap_ref[:, :hd] = gk.astype(F32).T.astype(BF16)
    gap_ref[:, hd:] = gv.astype(F32).T.astype(BF16)


def input_kernel(ids_ref, wq_ref, wh_ref, gq_ref, kvt_ref, mine_ref, other_ref):
    gq, kvt = gq_ref[...], kvt_ref[...]
    for out_ref, c in ((other_ref, 1 - ids_ref[OC]), (mine_ref, ids_ref[OC])):
        for y in range(8):
            for zh in range(2):
                cut = aligned(zh * 16 + y * 2 + c, 128)
                part = dot(gq, wq_ref[cut, :], ((1,), (1,))) + dot(kvt, wh_ref[:, cut], ((1,), (0,)))
                out_ref[y, zh] = part.astype(BF16)


def row_of(yl, c):
    return ((yl & 1) * 2 + c) * 2 + (yl >> 1)


def weight_kernel(ids_ref, x_ref, go_ref, o_ref, gq_ref, g0_ref, g1_ref, g3_ref, low_ref, high_ref):
    gq, out = gq_ref[...], o_ref[...]
    for s, refs in ((2, (low_ref, high_ref)), (1, (g1_ref,)), (3, (g3_ref,)), (0, (g0_ref,))):
        x = (ids_ref[OX] + s) & 3
        for yl in range(4):
            for c in range(2):
                row, block = row_of(yl, c), x * 8 + yl * 2 + c
                ref = refs[row // 4 if s == 2 else 0]
                row = row % 4 if s == 2 else row
                ref[row, 0:128, :] = dot(x_ref[block], gq, ((0,), (0,))).astype(BF16)
                ref[row, 128:256, :] = dot(out, go_ref[:, aligned(block, 128)], ((0,), (0,))).astype(BF16)


def half_kernel(mine_ref, theirs_ref, low_ref, high_ref, out_ref):
    out_ref[...] = (mine_ref[...].astype(F32) + theirs_ref[...].astype(F32)).astype(BF16)


def kv_kernel(ids_ref, x_ref, kvt_ref, *out_refs):
    kvg = jnp.sum(kvt_ref[...].astype(F32), axis=0).astype(BF16)
    for s in range(4):
        x = (ids_ref[OX] + s) & 3
        for yl in range(4):
            for c in range(2):
                part = dot(kvg, x_ref[x * 8 + yl * 2 + c], ((1,), (0,)))
                out_refs[s][row_of(yl, c)] = part.astype(BF16)


def fold_kernel(g1_ref, g3_ref, low_ref, high_ref, k1_ref, k3_ref, h1_ref, h3_ref):
    h1_ref[0:4, 0:256, :] = (g1_ref[0:4].astype(F32) + low_ref[...].astype(F32)).astype(BF16)
    h1_ref[4:8, 0:256, :] = g1_ref[4:8]
    h1_ref[:, 256:288, :] = k1_ref[...]
    h3_ref[0:4, 0:256, :] = g3_ref[0:4]
    h3_ref[4:8, 0:256, :] = (g3_ref[4:8].astype(F32) + high_ref[...].astype(F32)).astype(BF16)
    h3_ref[:, 256:288, :] = k3_ref[...]


def sum_kernel(g0_ref, k0_ref, k2_ref, h1_ref, h3_ref, out_ref):
    both = h1_ref[...].astype(F32) + h3_ref[...].astype(F32)
    out_ref[:, 0:256, :] = (g0_ref[...].astype(F32) + both[:, 0:256]).astype(BF16)
    out_ref[:, 256:288, :] = (k0_ref[...].astype(F32) + k2_ref[...].astype(F32) + both[:, 256:288]).astype(BF16)


def body(x_source, grad_out, w_query, w_kv, w_out, lengths, dest):
    groups, seq_total = dest.shape
    rows = grad_out.shape[0]
    longest = rows // seq_total
    vmem = pl.BlockSpec(memory_space=pltpu.VMEM)
    smem = pl.BlockSpec(memory_space=pltpu.SMEM)
    anyw = pl.BlockSpec(memory_space=pl.ANY)
    params = pltpu.CompilerParams(vmem_limit_bytes=32 * 1024 * 1024)
    shape = jax.ShapeDtypeStruct
    own_x, own_c, own_yl = lax.axis_index("x"), lax.axis_index("c"), lax.axis_index("yl")
    own_zh, own_zb = lax.axis_index("zh"), lax.axis_index("zb")
    ids = jnp.stack([lax.axis_index(DP), own_x, own_c, own_yl, own_zh]).astype(jnp.int32)

    def call(kernel, ins, outs, out_shape, **extra):
        return pl.pallas_call(
            kernel, out_shape=out_shape, in_specs=ins, out_specs=outs, compiler_params=params, **extra
        )

    outgoing = call(outgoing_kernel, [smem] * 3 + [vmem], vmem, shape((groups, longest, 128), BF16))(
        ids, lengths, dest, x_source
    )
    received = lax.all_to_all(outgoing, DP, 0, 0, tiled=True)
    w_own = w_kv.T
    w_parts = [w_own] + [lax.ppermute(w_own, "yl", [(i, i ^ s) for i in range(4)]) for s in (1, 2, 3)]
    grad_att = dot(grad_out, w_out, ((1,), (1,))).astype(BF16)

    eighth = shape((8, rows, 128), BF16)
    x_slice, spread = call(
        incoming_kernel, [smem] * 2 + [vmem] + [anyw] * 2, (vmem,) * 2, (shape((rows, 128), BF16), eighth)
    )(ids, dest, received, *w_parts[1:3])
    x_other = lax.ppermute(x_slice, "zh", SWAP)
    w_stack = call(stack_kernel, [vmem] * 4 + [anyw], vmem, shape((4,) + w_own.shape, BF16))(*w_parts, x_other)
    w_there = lax.ppermute(w_stack, "c", SWAP)
    w_head = call(head_kernel, [smem] + [vmem] * 2, vmem, shape((256, w_kv.shape[0]), BF16))(
        ids, w_stack, w_there
    )
    x_own = lax.all_to_all(spread, YY, 0, 0, tiled=True)
    x_own_there = lax.ppermute(x_own, "c", SWAP)
    x_other = lax.all_to_all(jnp.broadcast_to(x_other[None], (8, rows, 128)), YY, 0, 0, tiled=True)
    x_other_there = lax.ppermute(x_other, "c", SWAP)

    cosine, sine = tables(longest, seq_total, 128)
    out, gq, kv_term, kv_turned, x_all = call(
        lambda *refs: attention_kernel(longest, *refs),
        [smem] * 3 + [vmem] * 11,
        (vmem,) * 5,
        (
            shape((rows, 128), BF16),
            shape((rows, 128), BF16),
            shape((256, rows), BF16),
            shape((rows, 256), BF16),
            shape((32, rows, 128), BF16),
        ),
    )(
        ids, lengths, dest, x_own, x_other, x_own_there, x_other_there, w_query, w_head, grad_att,
        cosine, sine, cosine.T.copy(), sine.T.copy(),
    )
    kv_terms = lax.all_to_all(kv_term.reshape(8, 32, rows), PEERS, 0, 0, tiled=True)

    half = shape((8, 2, rows, 128), BF16)
    mine, other = call(input_kernel, [smem] + [vmem] * 4, (vmem,) * 2, (half, half))(
        ids, w_query, w_head, gq, kv_turned
    )
    theirs = lax.ppermute(other, "c", SWAP)
    full, quad = shape((8, 256, 128), BF16), shape((4, 256, 128), BF16)
    g0, g1, g3, low, high = call(
        weight_kernel, [smem] + [vmem] * 4, (vmem,) * 5, (full, full, full, quad, quad)
    )(ids, x_all, grad_out, out, gq)
    around = [[(i, (i + s) % 4) for i in range(4)] for s in range(4)]
    low = lax.ppermute(low, "x", around[1])
    high = lax.ppermute(high, "x", around[3])
    part = call(half_kernel, [vmem] * 2 + [anyw] * 2, vmem, half)(mine, theirs, low, high)
    k0, k1, k2, k3 = call(kv_kernel, [smem] + [vmem] * 2, (vmem,) * 4, (shape((8, 32, 128), BF16),) * 4)(
        ids, x_all, kv_terms
    )
    part = lax.all_to_all(part, YY, 0, 0, tiled=True)
    part = jnp.sum(part.astype(F32), axis=0)
    keep = jnp.where(own_zh == 0, part[0], part[1])
    send = jnp.where(own_zh == 0, part[1], part[0]).astype(BF16)
    grad_input = (keep + lax.ppermute(send, "zh", SWAP).astype(F32)).astype(BF16)

    most = shape((8, 288, 128), BF16)
    h1, h3 = call(fold_kernel, [vmem] * 6, (vmem,) * 2, (most, most))(g1, g3, low, high, k1, k3)
    h1, h3 = lax.ppermute(h1, "x", around[1]), lax.ppermute(h3, "x", around[3])
    k2 = lax.ppermute(k2, "x", around[2])
    total = call(sum_kernel, [vmem] * 5, vmem, most)(g0, k0, k2, h1, h3)
    total = lax.all_to_all(total.reshape(4, 576, 128), "za", 0, 0, tiled=True)
    total = jnp.sum(total.astype(F32), axis=0).reshape(2, 288, 128)
    keep = jnp.where(own_zb == 0, total[0], total[1])
    send = jnp.where(own_zb == 0, total[1], total[0]).astype(BF16)
    total = keep + lax.ppermute(send, "zb", SWAP).astype(F32)
    return grad_input, total[:128], total[256:].T, total[128:256]


def solution(mesh):
    fine = Mesh(mesh.devices.reshape(SIZES), AXES)
    placed = (P(DP, TP), P(DP, None), P(None, TP), P(None, TP), P(TP, None), P(), P())
    return jax.shard_map(
        body,
        mesh=fine,
        in_specs=placed,
        out_specs=(P(DP, TP), P(DP, TP), P(DP, TP), P(TP, DP)),
        check_vma=False,
    )
```

```python
import math

import jax
import jax.numpy as jnp
import numpy as np
from jax import lax
from jax.experimental import pallas as pl
from jax.experimental.pallas import tpu as pltpu
from jax.sharding import Mesh
from jax.sharding import PartitionSpec as P

AXES = ("x", "zb", "za", "zh", "yh", "yl", "c")
SIZES = (4, 2, 4, 2, 2, 4, 2)
DP = ("x", "zb", "za")
YY = ("yh", "yl")
TP = ("zh", "yh", "yl", "c")
PEERS = ("yl", "c")
F32 = jnp.float32
BF16 = jnp.bfloat16
SWAP = [(0, 1), (1, 0)]
G, OX, OC, OYL, OZH = 0, 1, 2, 3, 4


def dot(left, right, dims):
    return lax.dot_general(left, right, (dims, ((), ())), preferred_element_type=F32)


def tables(longest, seq_total, head_dim):
    frequency = np.exp(
        np.arange(head_dim // 2, dtype=np.float32) * np.float32(-2.0 * math.log(1000000.0) / head_dim)
    ).astype(np.float32)
    angles = (np.arange(longest, dtype=np.float32)[:, None] * frequency).astype(np.float32)
    cosine, sine = np.cos(angles), np.sin(angles)
    cosine = np.tile(np.concatenate([cosine, cosine], -1), (seq_total, 1)).astype(np.float32)
    signed = np.tile(np.concatenate([-sine, sine], -1), (seq_total, 1)).astype(np.float32)
    return cosine, signed


def aligned(index, size):
    return pl.ds(pl.multiple_of(index * size, size), size)


def incoming(ids_ref, dest_ref):
    groups, seq_total = dest_ref.shape
    senders = [lax.rem(ids_ref[G] + groups - dest_ref[0, j], groups) for j in range(seq_total)]
    ranks = []
    for j in range(seq_total):
        rank = jnp.int32(0)
        for i in range(seq_total):
            rank = rank + (senders[i] < senders[j]).astype(jnp.int32)
        ranks.append(rank)
    return senders, ranks


def outgoing_kernel(ids_ref, len_ref, dest_ref, x_ref, out_ref):
    groups, seq_total = dest_ref.shape
    longest = out_ref.shape[1]
    tokens = x_ref.shape[0]
    group = ids_ref[G]
    out_ref[...] = jnp.zeros_like(out_ref)
    place = lax.broadcasted_iota(jnp.int32, (longest, tokens), 0)
    token = lax.broadcasted_iota(jnp.int32, (longest, tokens), 1)
    start = jnp.int32(0)
    for j in range(seq_total):
        size = len_ref[group, j]
        chosen = jnp.where((token == place + start) & (place < size), 1.0, 0.0).astype(BF16)
        to = lax.rem(group + dest_ref[0, j], groups)
        out_ref[to] = dot(chosen, x_ref[...], ((1,), (0,))).astype(BF16)
        start = start + size


def incoming_kernel(ids_ref, dest_ref, x_ref, *refs):
    out_ref = refs[-1]
    longest = x_ref.shape[1]
    senders, ranks = incoming(ids_ref, dest_ref)
    for sender, rank in zip(senders, ranks):
        out_ref[aligned(rank, longest), :] = x_ref[sender]


def spread_kernel(ids_ref, own_ref, other_ref, *refs):
    out_ref = refs[-1]
    zh = ids_ref[OZH]
    for i in range(out_ref.shape[0]):
        out_ref[i, zh] = own_ref[...]
        out_ref[i, 1 - zh] = other_ref[...]


def stack_kernel(*refs):
    out_ref = refs[-1]
    for rel in range(4):
        out_ref[rel] = refs[rel][...]


def head_kernel(ids_ref, here_ref, there_ref, out_ref):
    for rel in range(4):
        for flip, source in enumerate((here_ref, there_ref)):
            peer = (ids_ref[OYL] ^ rel) * 2 + (ids_ref[OC] ^ flip)
            out_ref[aligned(peer, 32), :] = source[rel]


def attention_kernel(longest, ids_ref, len_ref, dest_ref, xm_ref, xt_ref, wq_ref, wh_ref, ga_ref,
                     cos_ref, sin_ref, cost_ref, sint_ref, o_ref, gq_ref, kvg_ref, gap_ref, x_ref):
    rows, hd = ga_ref.shape
    inv_scale = 1.0 / math.sqrt(hd)

    def turn(v):
        return jnp.concatenate([v[:, hd // 2:], v[:, : hd // 2]], 1)

    def turn_t(v):
        return jnp.concatenate([v[hd // 2:], v[: hd // 2]], 0)

    q = jnp.zeros((rows, hd), F32)
    kv = jnp.zeros((2 * hd, rows), F32)
    for part_ref, core in ((xm_ref, ids_ref[OC]), (xt_ref, 1 - ids_ref[OC])):
        for y in range(8):
            for zh in range(2):
                block = zh * 16 + y * 2 + core
                cut = aligned(block, 128)
                xb = part_ref[y, zh]
                x_ref[block] = xb
                q = q + dot(xb, wq_ref[cut, :], ((1,), (0,)))
                kv = kv + dot(wh_ref[:, cut], xb, ((1,), (1,)))
    cosine, sine, cosine_t, sine_t = cos_ref[...], sin_ref[...], cost_ref[...], sint_ref[...]
    q = q.astype(BF16).astype(F32)
    q = (q * cosine + turn(q) * sine).astype(BF16)
    kv = kv.astype(BF16)
    k = kv[:hd].astype(F32)
    k = (k * cosine_t + turn_t(k) * sine_t).astype(BF16)
    v = kv[hd:]
    ga = ga_ref[...]
    qi = lax.broadcasted_iota(jnp.int32, (rows, rows), 0)
    ki = lax.broadcasted_iota(jnp.int32, (rows, rows), 1)
    ends = jnp.zeros((rows, rows), jnp.int32)
    starts = jnp.zeros((rows, rows), jnp.int32)
    senders, ranks = incoming(ids_ref, dest_ref)
    for j in range(rows // longest):
        first = ranks[j] * longest
        here = (qi >= first) & (qi < first + longest)
        starts = jnp.where(here, first, starts)
        ends = jnp.where(here, first + len_ref[senders[j], j], ends)
    allowed = (ki >= starts) & (ki <= qi) & (ki < ends)
    scores = jnp.where(allowed, dot(q, k, ((1,), (0,))) * inv_scale, -1e30)
    highest = jnp.max(scores, axis=1, keepdims=True)
    weights = jnp.where(allowed, jnp.exp(scores - highest), 0.0)
    probs = weights / jnp.sum(weights, axis=1, keepdims=True)
    probs = jnp.where(qi < ends, probs, 0.0)
    low = probs.astype(BF16)
    o_ref[...] = dot(low, v, ((1,), (1,))).astype(BF16)
    gp = dot(ga, v, ((1,), (0,)))
    centre = jnp.sum(probs * gp, axis=1, keepdims=True)
    gs = (probs * (gp - centre) * inv_scale).astype(BF16)
    gq = dot(gs, k, ((1,), (1,)))
    gq_ref[...] = (gq * cosine - turn(gq) * sine).astype(BF16)
    gk = dot(q, gs, ((0,), (0,)))
    gk = (gk * cosine_t - turn_t(gk) * sine_t).astype(BF16)
    gv = dot(ga, low, ((0,), (0,))).astype(BF16)
    kvg_ref[:hd, :] = gk
    kvg_ref[hd:, :] = gv
    gap_ref[:, :hd] = gk.astype(F32).T.astype(BF16)
    gap_ref[:, hd:] = gv.astype(F32).T.astype(BF16)


def input_kernel(ids_ref, wq_ref, wh_ref, gq_ref, kvt_ref, mine_ref, other_ref):
    gq, kvt = gq_ref[...], kvt_ref[...]
    for out_ref, c in ((other_ref, 1 - ids_ref[OC]), (mine_ref, ids_ref[OC])):
        for y in range(8):
            for zh in range(2):
                cut = aligned(zh * 16 + y * 2 + c, 128)
                part = dot(gq, wq_ref[cut, :], ((1,), (1,))) + dot(kvt, wh_ref[:, cut], ((1,), (0,)))
                out_ref[y, zh] = part.astype(BF16)


def row_of(yl, c):
    return ((yl & 1) * 2 + c) * 2 + (yl >> 1)


def weight_kernel(ids_ref, x_ref, go_ref, o_ref, gq_ref, kvt_ref, g0_ref, g1_ref, g3_ref, low_ref, high_ref):
    gq, out = gq_ref[...], o_ref[...]
    kvg = jnp.sum(kvt_ref[...].astype(F32), axis=0).astype(BF16)
    for s, refs in ((2, (low_ref, high_ref)), (1, (g1_ref,)), (3, (g3_ref,)), (0, (g0_ref,))):
        x = (ids_ref[OX] + s) & 3
        for yl in range(4):
            for c in range(2):
                row, block = row_of(yl, c), x * 8 + yl * 2 + c
                ref = refs[row // 4 if s == 2 else 0]
                row = row % 4 if s == 2 else row
                ref[row, 0:128, :] = dot(x_ref[block], gq, ((0,), (0,))).astype(BF16)
                ref[row, 128:256, :] = dot(out, go_ref[:, aligned(block, 128)], ((0,), (0,))).astype(BF16)
                ref[row, 256:288, :] = dot(kvg, x_ref[block], ((1,), (0,))).astype(BF16)


def half_kernel(mine_ref, theirs_ref, after_ref, out_ref):
    out_ref[...] = (mine_ref[...].astype(F32) + theirs_ref[...].astype(F32)).astype(BF16)


def fold_kernel(g1_ref, g3_ref, low_ref, high_ref, h1_ref, h3_ref):
    h1_ref[0:4] = (g1_ref[0:4].astype(F32) + low_ref[...].astype(F32)).astype(BF16)
    h1_ref[4:8] = g1_ref[4:8]
    h3_ref[0:4] = g3_ref[0:4]
    h3_ref[4:8] = (g3_ref[4:8].astype(F32) + high_ref[...].astype(F32)).astype(BF16)


def sum_kernel(g0_ref, h1_ref, h3_ref, out_ref):
    out_ref[...] = sum(ref[...].astype(F32) for ref in (g0_ref, h1_ref, h3_ref)).astype(BF16)


def body(x_source, grad_out, w_query, w_kv, w_out, lengths, dest):
    groups, seq_total = dest.shape
    rows = grad_out.shape[0]
    longest = rows // seq_total
    vmem = pl.BlockSpec(memory_space=pltpu.VMEM)
    smem = pl.BlockSpec(memory_space=pltpu.SMEM)
    anyw = pl.BlockSpec(memory_space=pl.ANY)
    params = pltpu.CompilerParams(vmem_limit_bytes=32 * 1024 * 1024)
    shape = jax.ShapeDtypeStruct
    own_x, own_c, own_yl = lax.axis_index("x"), lax.axis_index("c"), lax.axis_index("yl")
    own_zh, own_zb = lax.axis_index("zh"), lax.axis_index("zb")
    ids = jnp.stack([lax.axis_index(DP), own_x, own_c, own_yl, own_zh]).astype(jnp.int32)

    def call(kernel, ins, outs, out_shape, micros=1):
        cost = pl.CostEstimate(flops=micros * 10**9, bytes_accessed=micros * 3_600_000, transcendentals=0)
        return pl.pallas_call(
            kernel, out_shape=out_shape, in_specs=ins, out_specs=outs, compiler_params=params, cost_estimate=cost
        )

    outgoing = call(outgoing_kernel, [smem] * 3 + [vmem], vmem, shape((groups, longest, 128), BF16))(
        ids, lengths, dest, x_source
    )
    received = lax.all_to_all(outgoing, DP, 0, 0, tiled=True)
    w_own = w_kv.T
    across = [[(i, i ^ s) for i in range(4)] for s in range(4)]
    w_parts = [w_own] + [lax.ppermute(w_own, "yl", across[s]) for s in (1, 2, 3)]
    grad_att = dot(grad_out, w_out, ((1,), (1,))).astype(BF16)

    half = shape((8, 2, rows, 128), BF16)
    x_slice = call(incoming_kernel, [smem] * 2 + [vmem, anyw], vmem, shape((rows, 128), BF16))(
        ids, dest, received, w_parts[1]
    )
    x_other = lax.ppermute(x_slice, "zh", SWAP)
    spread = call(spread_kernel, [smem] + [vmem] * 2 + [anyw] * 2, vmem, half)(ids, x_slice, x_other, *w_parts[2:])
    x_mine = lax.all_to_all(spread, YY, 0, 0, tiled=True)
    x_there = lax.ppermute(x_mine, "c", SWAP)
    w_stack = call(stack_kernel, [vmem] * 4 + [anyw], vmem, shape((4,) + w_own.shape, BF16))(*w_parts, spread)
    w_there = lax.ppermute(w_stack, "c", SWAP)
    w_head = call(head_kernel, [smem] + [vmem] * 2, vmem, shape((256, w_kv.shape[0]), BF16))(
        ids, w_stack, w_there
    )

    cosine, sine = tables(longest, seq_total, 128)
    out, gq, kv_term, kv_turned, x_all = call(
        lambda *refs: attention_kernel(longest, *refs),
        [smem] * 3 + [vmem] * 9,
        (vmem,) * 5,
        (
            shape((rows, 128), BF16),
            shape((rows, 128), BF16),
            shape((256, rows), BF16),
            shape((rows, 256), BF16),
            shape((32, rows, 128), BF16),
        ),
    )(
        ids, lengths, dest, x_mine, x_there, w_query, w_head, grad_att,
        cosine, sine, cosine.T.copy(), sine.T.copy(),
    )
    kv_terms = lax.all_to_all(kv_term.reshape(8, 32, rows), PEERS, 0, 0, tiled=True)

    mine, other = call(input_kernel, [smem] + [vmem] * 4, (vmem,) * 2, (half, half), 3)(
        ids, w_query, w_head, gq, kv_turned
    )
    theirs = lax.ppermute(other, "c", SWAP)
    full, quad = shape((8, 288, 128), BF16), shape((4, 288, 128), BF16)
    g0, g1, g3, low, high = call(
        weight_kernel, [smem] + [vmem] * 5, (vmem,) * 5, (full, full, full, quad, quad)
    )(ids, x_all, grad_out, out, gq, kv_terms)
    around = [[(i, (i + s) % 4) for i in range(4)] for s in range(4)]
    low = lax.ppermute(low, "x", around[1])
    high = lax.ppermute(high, "x", around[3])
    h1, h3 = call(fold_kernel, [vmem] * 4, (vmem,) * 2, (full, full))(g1, g3, low, high)
    h1, h3 = lax.ppermute(h1, "x", around[1]), lax.ppermute(h3, "x", around[3])
    total = call(sum_kernel, [vmem] * 3, vmem, full)(g0, h1, h3)

    part = call(half_kernel, [vmem] * 2 + [anyw], vmem, half)(mine, theirs, g0)
    part = lax.all_to_all(part, YY, 0, 0, tiled=True)
    part = jnp.sum(part.astype(F32), axis=0)
    keep = jnp.where(own_zh == 0, part[0], part[1])
    send = jnp.where(own_zh == 0, part[1], part[0]).astype(BF16)
    grad_input = (keep + lax.ppermute(send, "zh", SWAP).astype(F32)).astype(BF16)

    total = lax.all_to_all(total.reshape(4, 576, 128), "za", 0, 0, tiled=True)
    total = jnp.sum(total.astype(F32), axis=0).reshape(2, 288, 128)
    keep = jnp.where(own_zb == 0, total[0], total[1])
    send = jnp.where(own_zb == 0, total[1], total[0]).astype(BF16)
    total = keep + lax.ppermute(send, "zb", SWAP).astype(F32)
    return grad_input, total[:128], total[256:].T, total[128:256]


def solution(mesh):
    fine = Mesh(mesh.devices.reshape(SIZES), AXES)
    placed = (P(DP, TP), P(DP, None), P(None, TP), P(None, TP), P(TP, None), P(), P())
    return jax.shard_map(
        body,
        mesh=fine,
        in_specs=placed,
        out_specs=(P(DP, TP), P(DP, TP), P(DP, TP), P(TP, DP)),
        check_vma=False,
    )
```

```python
import math

import jax
import jax.numpy as jnp
import numpy as np
from jax import lax
from jax.experimental import pallas as pl
from jax.experimental.pallas import tpu as pltpu
from jax.sharding import Mesh
from jax.sharding import PartitionSpec as P

AXES = ("x", "zb", "za", "zh", "yh", "yl", "c")
SIZES = (4, 2, 4, 2, 2, 4, 2)
DP = ("x", "zb", "za")
YY = ("yh", "yl")
TP = ("zh", "yh", "yl", "c")
PEERS = ("yl", "c")
F32 = jnp.float32
BF16 = jnp.bfloat16
SWAP = [(0, 1), (1, 0)]
G, OX, OC, OYL, OZH, OYH, OZB = 0, 1, 2, 3, 4, 5, 6


def dot(left, right, dims):
    return lax.dot_general(left, right, (dims, ((), ())), preferred_element_type=F32)


def tables(longest, seq_total, head_dim):
    frequency = np.exp(
        np.arange(head_dim // 2, dtype=np.float32) * np.float32(-2.0 * math.log(1000000.0) / head_dim)
    ).astype(np.float32)
    angles = (np.arange(longest, dtype=np.float32)[:, None] * frequency).astype(np.float32)
    cosine, sine = np.cos(angles), np.sin(angles)
    cosine = np.tile(np.concatenate([cosine, cosine], -1), (seq_total, 1)).astype(np.float32)
    signed = np.tile(np.concatenate([-sine, sine], -1), (seq_total, 1)).astype(np.float32)
    return cosine, signed


def aligned(index, size):
    return pl.ds(pl.multiple_of(index * size, size), size)


def incoming(ids_ref, dest_ref):
    groups, seq_total = dest_ref.shape
    senders = [lax.rem(ids_ref[G] + groups - dest_ref[0, j], groups) for j in range(seq_total)]
    ranks = []
    for j in range(seq_total):
        rank = jnp.int32(0)
        for i in range(seq_total):
            rank = rank + (senders[i] < senders[j]).astype(jnp.int32)
        ranks.append(rank)
    return senders, ranks


def outgoing_kernel(ids_ref, len_ref, dest_ref, x_ref, out_ref):
    groups, seq_total = dest_ref.shape
    longest = out_ref.shape[1]
    tokens = x_ref.shape[0]
    group = ids_ref[G]
    out_ref[...] = jnp.zeros_like(out_ref)
    place = lax.broadcasted_iota(jnp.int32, (longest, tokens), 0)
    token = lax.broadcasted_iota(jnp.int32, (longest, tokens), 1)
    start = jnp.int32(0)
    for j in range(seq_total):
        size = len_ref[group, j]
        chosen = jnp.where((token == place + start) & (place < size), 1.0, 0.0).astype(BF16)
        to = lax.rem(group + dest_ref[0, j], groups)
        out_ref[to] = dot(chosen, x_ref[...], ((1,), (0,))).astype(BF16)
        start = start + size


def incoming_kernel(ids_ref, dest_ref, x_ref, *refs):
    out_ref = refs[-1]
    longest = x_ref.shape[1]
    senders, ranks = incoming(ids_ref, dest_ref)
    for sender, rank in zip(senders, ranks):
        out_ref[aligned(rank, longest), :] = x_ref[sender]


def spread_kernel(ids_ref, own_ref, other_ref, *refs):
    out_ref = refs[-1]
    zh = ids_ref[OZH]
    for i in range(out_ref.shape[0]):
        out_ref[i, zh] = own_ref[...]
        out_ref[i, 1 - zh] = other_ref[...]


def stack_kernel(*refs):
    out_ref = refs[-1]
    for rel in range(4):
        out_ref[rel] = refs[rel][...]


def head_kernel(ids_ref, here_ref, there_ref, out_ref):
    for rel in range(4):
        for flip, source in enumerate((here_ref, there_ref)):
            peer = (ids_ref[OYL] ^ rel) * 2 + (ids_ref[OC] ^ flip)
            out_ref[aligned(peer, 32), :] = source[rel]


def attention_kernel(longest, ids_ref, len_ref, dest_ref, xm_ref, xt_ref, wq_ref, wh_ref, ga_ref,
                     cos_ref, sin_ref, cost_ref, sint_ref, o_ref, gq_ref, kvg_ref, gap_ref, x_ref):
    rows, hd = ga_ref.shape
    inv_scale = 1.0 / math.sqrt(hd)

    def turn(v):
        return jnp.concatenate([v[:, hd // 2:], v[:, : hd // 2]], 1)

    def turn_t(v):
        return jnp.concatenate([v[hd // 2:], v[: hd // 2]], 0)

    q = jnp.zeros((rows, hd), F32)
    kv = jnp.zeros((2 * hd, rows), F32)
    for part_ref, core in ((xm_ref, ids_ref[OC]), (xt_ref, 1 - ids_ref[OC])):
        for y in range(8):
            for zh in range(2):
                block = zh * 16 + y * 2 + core
                cut = aligned(block, 128)
                xb = part_ref[y, zh]
                x_ref[block] = xb
                q = q + dot(xb, wq_ref[cut, :], ((1,), (0,)))
                kv = kv + dot(wh_ref[:, cut], xb, ((1,), (1,)))
    cosine, sine, cosine_t, sine_t = cos_ref[...], sin_ref[...], cost_ref[...], sint_ref[...]
    q = q.astype(BF16).astype(F32)
    q = (q * cosine + turn(q) * sine).astype(BF16)
    kv = kv.astype(BF16)
    k = kv[:hd].astype(F32)
    k = (k * cosine_t + turn_t(k) * sine_t).astype(BF16)
    v = kv[hd:]
    ga = ga_ref[...]
    qi = lax.broadcasted_iota(jnp.int32, (rows, rows), 0)
    ki = lax.broadcasted_iota(jnp.int32, (rows, rows), 1)
    ends = jnp.zeros((rows, rows), jnp.int32)
    starts = jnp.zeros((rows, rows), jnp.int32)
    senders, ranks = incoming(ids_ref, dest_ref)
    for j in range(rows // longest):
        first = ranks[j] * longest
        here = (qi >= first) & (qi < first + longest)
        starts = jnp.where(here, first, starts)
        ends = jnp.where(here, first + len_ref[senders[j], j], ends)
    allowed = (ki >= starts) & (ki <= qi) & (ki < ends)
    scores = jnp.where(allowed, dot(q, k, ((1,), (0,))) * inv_scale, -1e30)
    highest = jnp.max(scores, axis=1, keepdims=True)
    weights = jnp.where(allowed, jnp.exp(scores - highest), 0.0)
    probs = weights / jnp.sum(weights, axis=1, keepdims=True)
    probs = jnp.where(qi < ends, probs, 0.0)
    low = probs.astype(BF16)
    o_ref[...] = dot(low, v, ((1,), (1,))).astype(BF16)
    gp = dot(ga, v, ((1,), (0,)))
    centre = jnp.sum(probs * gp, axis=1, keepdims=True)
    gs = (probs * (gp - centre) * inv_scale).astype(BF16)
    gq = dot(gs, k, ((1,), (1,)))
    gq_ref[...] = (gq * cosine - turn(gq) * sine).astype(BF16)
    gk = dot(q, gs, ((0,), (0,)))
    gk = (gk * cosine_t - turn_t(gk) * sine_t).astype(BF16)
    gv = dot(ga, low, ((0,), (0,))).astype(BF16)
    kvg_ref[:hd, :] = gk
    kvg_ref[hd:, :] = gv
    gap_ref[:, :hd] = gk.astype(F32).T.astype(BF16)
    gap_ref[:, hd:] = gv.astype(F32).T.astype(BF16)


def input_kernel(ids_ref, wq_ref, wh_ref, gq_ref, kvt_ref, term_ref, mine_ref, other_ref):
    gq, kvt = gq_ref[...], kvt_ref[...]
    for out_ref, c in ((other_ref, 1 - ids_ref[OC]), (mine_ref, ids_ref[OC])):
        for y in range(8):
            for zh in range(2):
                cut = aligned(zh * 16 + y * 2 + c, 128)
                part = dot(gq, wq_ref[cut, :], ((1,), (1,))) + dot(kvt, wh_ref[:, cut], ((1,), (0,)))
                out_ref[y, zh * 128 : zh * 128 + 128, :] = part.astype(BF16)
            term = term_ref[aligned((y & 3) * 2 + c, 32), :]
            out_ref[y, 256:288, :] = jnp.where(ids_ref[OYH] == y >> 2, term, jnp.zeros_like(term))


def row_of(yl, c):
    return ((yl & 1) * 2 + c) * 2 + (yl >> 1)


def weight_kernel(ids_ref, x_ref, go_ref, o_ref, gq_ref, after_ref, g0_ref, g1_ref, g3_ref, low_ref, high_ref):
    gq, out = gq_ref[...], o_ref[...]
    for s, refs in ((2, (low_ref, high_ref)), (1, (g1_ref,)), (3, (g3_ref,)), (0, (g0_ref,))):
        x = (ids_ref[OX] + s) & 3
        for yl in range(4):
            for c in range(2):
                row, block = row_of(yl, c), x * 8 + yl * 2 + c
                ref = refs[row // 4 if s == 2 else 0]
                row = row % 4 if s == 2 else row
                ref[row, 0:128, :] = dot(x_ref[block], gq, ((0,), (0,))).astype(BF16)
                ref[row, 128:256, :] = dot(out, go_ref[:, aligned(block, 128)], ((0,), (0,))).astype(BF16)


def half_kernel(mine_ref, theirs_ref, out_ref):
    out_ref[...] = (mine_ref[...].astype(F32) + theirs_ref[...].astype(F32)).astype(BF16)


def collect_kernel(ids_ref, part_ref, x_ref, keep_ref, send_ref, *k_refs):
    total = jnp.sum(part_ref[...].astype(F32), axis=0)
    first = ids_ref[OZH] == 0
    keep_ref[...] = jnp.where(first, total[:128], total[128:256])
    send_ref[...] = jnp.where(first, total[128:256], total[:128]).astype(BF16)
    kvg = total[256:288].astype(BF16)
    for s in (1, 2, 3, 0):
        x = (ids_ref[OX] + s) & 3
        for yl in range(4):
            for c in range(2):
                k_refs[s][row_of(yl, c)] = dot(kvg, x_ref[x * 8 + yl * 2 + c], ((1,), (0,))).astype(BF16)


def fold_kernel(g1_ref, g3_ref, low_ref, high_ref, h1_ref, h3_ref):
    h1_ref[0:4] = (g1_ref[0:4].astype(F32) + low_ref[...].astype(F32)).astype(BF16)
    h1_ref[4:8] = g1_ref[4:8]
    h3_ref[0:4] = g3_ref[0:4]
    h3_ref[4:8] = (g3_ref[4:8].astype(F32) + high_ref[...].astype(F32)).astype(BF16)


def sum_kernel(*refs):
    send_ref, out_ref, late_ref = refs[7:]
    out_ref[:, 0:256, :] = sum(ref[...].astype(F32) for ref in refs[:3]).astype(BF16)
    out_ref[:, 256:288, :] = sum(ref[...].astype(F32) for ref in refs[3:7]).astype(BF16)
    late_ref[...] = send_ref[...]


def last_kernel(ids_ref, total_ref, there_ref, query_ref, wout_ref, kv_ref):
    own = total_ref[ids_ref[OZB]] + there_ref[...].astype(F32)
    query_ref[...] = own[0:128]
    wout_ref[...] = own[128:256]
    kv_ref[...] = own[256:288]


def body(x_source, grad_out, w_query, w_kv, w_out, lengths, dest):
    groups, seq_total = dest.shape
    rows = grad_out.shape[0]
    longest = rows // seq_total
    vmem = pl.BlockSpec(memory_space=pltpu.VMEM)
    smem = pl.BlockSpec(memory_space=pltpu.SMEM)
    anyw = pl.BlockSpec(memory_space=pl.ANY)
    params = pltpu.CompilerParams(vmem_limit_bytes=32 * 1024 * 1024)
    shape = jax.ShapeDtypeStruct
    own_x, own_c, own_yl = lax.axis_index("x"), lax.axis_index("c"), lax.axis_index("yl")
    own_zh, own_zb = lax.axis_index("zh"), lax.axis_index("zb")
    ids = jnp.stack([lax.axis_index(DP), own_x, own_c, own_yl, own_zh, lax.axis_index("yh"), own_zb]).astype(jnp.int32)

    def call(kernel, ins, outs, out_shape, micros=1):
        cost = pl.CostEstimate(flops=micros * 10**9, bytes_accessed=micros * 3_600_000, transcendentals=0)
        return pl.pallas_call(
            kernel, out_shape=out_shape, in_specs=ins, out_specs=outs, compiler_params=params, cost_estimate=cost
        )

    outgoing = call(outgoing_kernel, [smem] * 3 + [vmem], vmem, shape((groups, longest, 128), BF16))(
        ids, lengths, dest, x_source
    )
    received = lax.all_to_all(outgoing, DP, 0, 0, tiled=True)
    w_own = w_kv.T
    across = [[(i, i ^ s) for i in range(4)] for s in range(4)]
    w_parts = [w_own] + [lax.ppermute(w_own, "yl", across[s]) for s in (1, 2, 3)]
    grad_att = dot(grad_out, w_out, ((1,), (1,))).astype(BF16)

    half = shape((8, 2, rows, 128), BF16)
    x_slice = call(incoming_kernel, [smem] * 2 + [vmem, anyw, anyw], vmem, shape((rows, 128), BF16))(
        ids, dest, received, w_parts[1], grad_att
    )
    x_other = lax.ppermute(x_slice, "zh", SWAP)
    spread = call(spread_kernel, [smem] + [vmem] * 2 + [anyw] * 2, vmem, half)(ids, x_slice, x_other, *w_parts[2:])
    x_mine = lax.all_to_all(spread, YY, 0, 0, tiled=True)
    x_there = lax.ppermute(x_mine, "c", SWAP)
    w_stack = call(stack_kernel, [vmem] * 4 + [anyw], vmem, shape((4,) + w_own.shape, BF16))(*w_parts, spread)
    w_there = lax.ppermute(w_stack, "c", SWAP)
    w_head = call(head_kernel, [smem] + [vmem] * 2, vmem, shape((256, w_kv.shape[0]), BF16))(
        ids, w_stack, w_there
    )

    cosine, sine = tables(longest, seq_total, 128)
    out, gq, kv_term, kv_turned, x_all = call(
        lambda *refs: attention_kernel(longest, *refs),
        [smem] * 3 + [vmem] * 9,
        (vmem,) * 5,
        (
            shape((rows, 128), BF16),
            shape((rows, 128), BF16),
            shape((256, rows), BF16),
            shape((rows, 256), BF16),
            shape((32, rows, 128), BF16),
        ),
    )(
        ids, lengths, dest, x_mine, x_there, w_query, w_head, grad_att,
        cosine, sine, cosine.T.copy(), sine.T.copy(),
    )

    most, full = shape((8, 288, 128), BF16), shape((8, 256, 128), BF16)
    quad, slim, block = shape((4, 256, 128), BF16), shape((8, 32, 128), BF16), (rows, 128)
    mine, other = call(input_kernel, [smem] + [vmem] * 5, (vmem,) * 2, (most, most), 3)(
        ids, w_query, w_head, gq, kv_turned, kv_term
    )
    theirs = lax.ppermute(other, "c", SWAP)
    part = call(half_kernel, [vmem] * 2, vmem, most)(mine, theirs)
    around = [[(i, (i + s) % 4) for i in range(4)] for s in range(4)]
    g0, g1, g3, low, high = call(
        weight_kernel, [smem] + [vmem] * 4 + [anyw], (vmem,) * 5, (full, full, full, quad, quad)
    )(ids, x_all, grad_out, out, gq, part)
    part = lax.all_to_all(part, YY, 0, 0, tiled=True)
    low = lax.ppermute(low, "x", around[1])
    high = lax.ppermute(high, "x", around[3])
    h1, h3 = call(fold_kernel, [vmem] * 4, (vmem,) * 2, (full, full))(g1, g3, low, high)
    h1, h3 = lax.ppermute(h1, "x", around[1]), lax.ppermute(h3, "x", around[3])
    keep, send, *ks = call(
        collect_kernel, [smem] + [vmem] * 2, (vmem,) * 6, (shape(block, F32), shape(block, BF16)) + (slim,) * 4
    )(ids, part, x_all)
    ks = ks[:1] + [lax.ppermute(ks[s], "x", around[s]) for s in (1, 2, 3)]
    total, send = call(sum_kernel, [vmem] * 8, (vmem,) * 2, (most, shape(block, BF16)))(g0, h1, h3, *ks, send)
    grad_input = (keep + lax.ppermute(send, "zh", SWAP).astype(F32)).astype(BF16)

    total = lax.all_to_all(total.reshape(4, 576, 128), "za", 0, 0, tiled=True)
    total = jnp.sum(total.astype(F32), axis=0).reshape(2, 288, 128)
    send = jnp.where(own_zb == 0, total[1], total[0]).astype(BF16)
    query, wout, kv = call(
        last_kernel, [smem] + [vmem] * 2, (vmem,) * 3, (shape(block, F32), shape(block, F32), shape((32, 128), F32))
    )(ids, total, lax.ppermute(send, "zb", SWAP))
    return grad_input, query, kv.T, wout


def solution(mesh):
    fine = Mesh(mesh.devices.reshape(SIZES), AXES)
    placed = (P(DP, TP), P(DP, None), P(None, TP), P(None, TP), P(TP, None), P(), P())
    return jax.shard_map(
        body,
        mesh=fine,
        in_specs=placed,
        out_specs=(P(DP, TP), P(DP, TP), P(DP, TP), P(TP, DP)),
        check_vma=False,
    )
```

```python
import math

import jax
import jax.numpy as jnp
import numpy as np
from jax import lax
from jax.experimental import pallas as pl
from jax.experimental.pallas import tpu as pltpu
from jax.sharding import Mesh
from jax.sharding import PartitionSpec as P

AXES = ("x", "zb", "za", "zh", "yh", "yl", "c")
SIZES = (4, 2, 4, 2, 2, 4, 2)
DP = ("x", "zb", "za")
YY = ("yh", "yl")
TP = ("zh", "yh", "yl", "c")
PEERS = ("yl", "c")
F32 = jnp.float32
BF16 = jnp.bfloat16
SWAP = [(0, 1), (1, 0)]
G, OX, OC, OYL, OZH, OYH, OZB = 0, 1, 2, 3, 4, 5, 6


def dot(left, right, dims):
    return lax.dot_general(left, right, (dims, ((), ())), preferred_element_type=F32)


def tables(longest, seq_total, head_dim):
    frequency = np.exp(
        np.arange(head_dim // 2, dtype=np.float32) * np.float32(-2.0 * math.log(1000000.0) / head_dim)
    ).astype(np.float32)
    angles = (np.arange(longest, dtype=np.float32)[:, None] * frequency).astype(np.float32)
    cosine, sine = np.cos(angles), np.sin(angles)
    cosine = np.tile(np.concatenate([cosine, cosine], -1), (seq_total, 1)).astype(np.float32)
    signed = np.tile(np.concatenate([-sine, sine], -1), (seq_total, 1)).astype(np.float32)
    return cosine, signed


def aligned(index, size):
    return pl.ds(pl.multiple_of(index * size, size), size)


def incoming(ids_ref, dest_ref):
    groups, seq_total = dest_ref.shape
    senders = [lax.rem(ids_ref[G] + groups - dest_ref[0, j], groups) for j in range(seq_total)]
    ranks = []
    for j in range(seq_total):
        rank = jnp.int32(0)
        for i in range(seq_total):
            rank = rank + (senders[i] < senders[j]).astype(jnp.int32)
        ranks.append(rank)
    return senders, ranks


def outgoing_kernel(ids_ref, len_ref, dest_ref, x_ref, out_ref):
    groups, seq_total = dest_ref.shape
    longest = out_ref.shape[1]
    tokens = x_ref.shape[0]
    group = ids_ref[G]
    out_ref[...] = jnp.zeros_like(out_ref)
    place = lax.broadcasted_iota(jnp.int32, (longest, tokens), 0)
    token = lax.broadcasted_iota(jnp.int32, (longest, tokens), 1)
    start = jnp.int32(0)
    for j in range(seq_total):
        size = len_ref[group, j]
        chosen = jnp.where((token == place + start) & (place < size), 1.0, 0.0).astype(BF16)
        to = lax.rem(group + dest_ref[0, j], groups)
        out_ref[to] = dot(chosen, x_ref[...], ((1,), (0,))).astype(BF16)
        start = start + size


def incoming_kernel(ids_ref, dest_ref, x_ref, *refs):
    out_ref = refs[-1]
    longest = x_ref.shape[1]
    senders, ranks = incoming(ids_ref, dest_ref)
    for sender, rank in zip(senders, ranks):
        out_ref[aligned(rank, longest), :] = x_ref[sender]


def spread_kernel(ids_ref, own_ref, other_ref, *refs):
    out_ref = refs[-1]
    zh = ids_ref[OZH]
    for i in range(out_ref.shape[0]):
        out_ref[i, zh] = own_ref[...]
        out_ref[i, 1 - zh] = other_ref[...]


def stack_kernel(*refs):
    out_ref = refs[-1]
    for rel in range(4):
        out_ref[rel] = refs[rel][...]


def head_kernel(ids_ref, here_ref, there_ref, out_ref):
    for rel in range(4):
        for flip, source in enumerate((here_ref, there_ref)):
            peer = (ids_ref[OYL] ^ rel) * 2 + (ids_ref[OC] ^ flip)
            out_ref[aligned(peer, 32), :] = source[rel]


def attention_kernel(longest, ids_ref, len_ref, dest_ref, xm_ref, xt_ref, wq_ref, wh_ref, ga_ref,
                     cos_ref, sin_ref, cost_ref, sint_ref, o_ref, gq_ref, kvg_ref, gap_ref, x_ref):
    rows, hd = ga_ref.shape
    inv_scale = 1.0 / math.sqrt(hd)

    def turn(v):
        return jnp.concatenate([v[:, hd // 2:], v[:, : hd // 2]], 1)

    def turn_t(v):
        return jnp.concatenate([v[hd // 2:], v[: hd // 2]], 0)

    q = jnp.zeros((rows, hd), F32)
    kv = jnp.zeros((2 * hd, rows), F32)
    for part_ref, core in ((xm_ref, ids_ref[OC]), (xt_ref, 1 - ids_ref[OC])):
        for y in range(8):
            for zh in range(2):
                block = zh * 16 + y * 2 + core
                cut = aligned(block, 128)
                xb = part_ref[y, zh]
                x_ref[block] = xb
                q = q + dot(xb, wq_ref[cut, :], ((1,), (0,)))
                kv = kv + dot(wh_ref[:, cut], xb, ((1,), (1,)))
    cosine, sine, cosine_t, sine_t = cos_ref[...], sin_ref[...], cost_ref[...], sint_ref[...]
    q = q.astype(BF16).astype(F32)
    q = (q * cosine + turn(q) * sine).astype(BF16)
    kv = kv.astype(BF16)
    k = kv[:hd].astype(F32)
    k = (k * cosine_t + turn_t(k) * sine_t).astype(BF16)
    v = kv[hd:]
    ga = ga_ref[...]
    qi = lax.broadcasted_iota(jnp.int32, (rows, rows), 0)
    ki = lax.broadcasted_iota(jnp.int32, (rows, rows), 1)
    ends = jnp.zeros((rows, rows), jnp.int32)
    starts = jnp.zeros((rows, rows), jnp.int32)
    senders, ranks = incoming(ids_ref, dest_ref)
    for j in range(rows // longest):
        first = ranks[j] * longest
        here = (qi >= first) & (qi < first + longest)
        starts = jnp.where(here, first, starts)
        ends = jnp.where(here, first + len_ref[senders[j], j], ends)
    allowed = (ki >= starts) & (ki <= qi) & (ki < ends)
    scores = jnp.where(allowed, dot(q, k, ((1,), (0,))) * inv_scale, -1e30)
    highest = jnp.max(scores, axis=1, keepdims=True)
    weights = jnp.where(allowed, jnp.exp(scores - highest), 0.0)
    probs = weights / jnp.sum(weights, axis=1, keepdims=True)
    probs = jnp.where(qi < ends, probs, 0.0)
    low = probs.astype(BF16)
    o_ref[...] = dot(low, v, ((1,), (1,))).astype(BF16)
    gp = dot(ga, v, ((1,), (0,)))
    centre = jnp.sum(probs * gp, axis=1, keepdims=True)
    gs = (probs * (gp - centre) * inv_scale).astype(BF16)
    gq = dot(gs, k, ((1,), (1,)))
    gq_ref[...] = (gq * cosine - turn(gq) * sine).astype(BF16)
    gk = dot(q, gs, ((0,), (0,)))
    gk = (gk * cosine_t - turn_t(gk) * sine_t).astype(BF16)
    gv = dot(ga, low, ((0,), (0,))).astype(BF16)
    kvg_ref[:hd, :] = gk
    kvg_ref[hd:, :] = gv
    gap_ref[:, :hd] = gk.astype(F32).T.astype(BF16)
    gap_ref[:, hd:] = gv.astype(F32).T.astype(BF16)


def input_kernel(ids_ref, wq_ref, wh_ref, gq_ref, kvt_ref, term_ref, mine_ref, other_ref):
    gq, kvt = gq_ref[...], kvt_ref[...]
    for out_ref, c in ((other_ref, 1 - ids_ref[OC]), (mine_ref, ids_ref[OC])):
        for y in range(8):
            for zh in range(2):
                cut = aligned(zh * 16 + y * 2 + c, 128)
                part = dot(gq, wq_ref[cut, :], ((1,), (1,))) + dot(kvt, wh_ref[:, cut], ((1,), (0,)))
                out_ref[y, zh * 128 : zh * 128 + 128, :] = part.astype(BF16)
            term = term_ref[aligned((y & 3) * 2 + c, 32), :]
            out_ref[y, 256:288, :] = jnp.where(ids_ref[OYH] == y >> 2, term, jnp.zeros_like(term))


def row_of(yl, c):
    return ((yl & 1) * 2 + c) * 2 + (yl >> 1)


def weight_kernel(ids_ref, x_ref, go_ref, o_ref, gq_ref, g0_ref, g1_ref, g3_ref, low_ref, high_ref):
    gq, out = gq_ref[...], o_ref[...]
    for s, refs in ((2, (low_ref, high_ref)), (1, (g1_ref,)), (3, (g3_ref,)), (0, (g0_ref,))):
        x = (ids_ref[OX] + s) & 3
        for yl in range(4):
            for c in range(2):
                row, block = row_of(yl, c), x * 8 + yl * 2 + c
                ref = refs[row // 4 if s == 2 else 0]
                row = row % 4 if s == 2 else row
                ref[row, 0:128, :] = dot(x_ref[block], gq, ((0,), (0,))).astype(BF16)
                ref[row, 128:256, :] = dot(out, go_ref[:, aligned(block, 128)], ((0,), (0,))).astype(BF16)


def half_kernel(mine_ref, theirs_ref, after_ref, out_ref):
    out_ref[...] = (mine_ref[...].astype(F32) + theirs_ref[...].astype(F32)).astype(BF16)


def collect_kernel(ids_ref, part_ref, x_ref, keep_ref, send_ref, *k_refs):
    total = jnp.sum(part_ref[...].astype(F32), axis=0)
    first = ids_ref[OZH] == 0
    keep_ref[...] = jnp.where(first, total[:128], total[128:256])
    send_ref[...] = jnp.where(first, total[128:256], total[:128]).astype(BF16)
    kvg = total[256:288].astype(BF16)
    for s in (1, 2, 3, 0):
        x = (ids_ref[OX] + s) & 3
        for yl in range(4):
            for c in range(2):
                k_refs[s][row_of(yl, c)] = dot(kvg, x_ref[x * 8 + yl * 2 + c], ((1,), (0,))).astype(BF16)


def fold_kernel(g1_ref, g3_ref, low_ref, high_ref, h1_ref, h3_ref):
    h1_ref[0:4] = (g1_ref[0:4].astype(F32) + low_ref[...].astype(F32)).astype(BF16)
    h1_ref[4:8] = g1_ref[4:8]
    h3_ref[0:4] = g3_ref[0:4]
    h3_ref[4:8] = (g3_ref[4:8].astype(F32) + high_ref[...].astype(F32)).astype(BF16)


def sum_kernel(*refs):
    send_ref, out_ref, late_ref = refs[7:]
    out_ref[:, 0:256, :] = sum(ref[...].astype(F32) for ref in refs[:3]).astype(BF16)
    out_ref[:, 256:288, :] = sum(ref[...].astype(F32) for ref in refs[3:7]).astype(BF16)
    late_ref[...] = send_ref[...]


def last_kernel(ids_ref, total_ref, there_ref, query_ref, wout_ref, kv_ref):
    own = total_ref[ids_ref[OZB]] + there_ref[...].astype(F32)
    query_ref[...] = own[0:128]
    wout_ref[...] = own[128:256]
    kv_ref[...] = own[256:288]


def body(x_source, grad_out, w_query, w_kv, w_out, lengths, dest):
    groups, seq_total = dest.shape
    rows = grad_out.shape[0]
    longest = rows // seq_total
    vmem = pl.BlockSpec(memory_space=pltpu.VMEM)
    smem = pl.BlockSpec(memory_space=pltpu.SMEM)
    anyw = pl.BlockSpec(memory_space=pl.ANY)
    params = pltpu.CompilerParams(vmem_limit_bytes=32 * 1024 * 1024)
    shape = jax.ShapeDtypeStruct
    own_x, own_c, own_yl = lax.axis_index("x"), lax.axis_index("c"), lax.axis_index("yl")
    own_zh, own_zb = lax.axis_index("zh"), lax.axis_index("zb")
    ids = jnp.stack([lax.axis_index(DP), own_x, own_c, own_yl, own_zh, lax.axis_index("yh"), own_zb]).astype(jnp.int32)

    def call(kernel, ins, outs, out_shape, micros=1):
        cost = pl.CostEstimate(flops=micros * 10**9, bytes_accessed=micros * 3_600_000, transcendentals=0)
        return pl.pallas_call(
            kernel, out_shape=out_shape, in_specs=ins, out_specs=outs, compiler_params=params, cost_estimate=cost
        )

    outgoing = call(outgoing_kernel, [smem] * 3 + [vmem], vmem, shape((groups, longest, 128), BF16))(
        ids, lengths, dest, x_source
    )
    received = lax.all_to_all(outgoing, DP, 0, 0, tiled=True)
    w_own = w_kv.T
    across = [[(i, i ^ s) for i in range(4)] for s in range(4)]
    w_parts = [w_own] + [lax.ppermute(w_own, "yl", across[s]) for s in (1, 2, 3)]
    grad_att = dot(grad_out, w_out, ((1,), (1,))).astype(BF16)

    half = shape((8, 2, rows, 128), BF16)
    x_slice = call(incoming_kernel, [smem] * 2 + [vmem, anyw, anyw], vmem, shape((rows, 128), BF16))(
        ids, dest, received, w_parts[1], grad_att
    )
    x_other = lax.ppermute(x_slice, "zh", SWAP)
    spread = call(spread_kernel, [smem] + [vmem] * 2 + [anyw] * 2, vmem, half)(ids, x_slice, x_other, *w_parts[2:])
    x_mine = lax.all_to_all(spread, YY, 0, 0, tiled=True)
    x_there = lax.ppermute(x_mine, "c", SWAP)
    w_stack = call(stack_kernel, [vmem] * 4 + [anyw], vmem, shape((4,) + w_own.shape, BF16))(*w_parts, spread)
    w_there = lax.ppermute(w_stack, "c", SWAP)
    w_head = call(head_kernel, [smem] + [vmem] * 2, vmem, shape((256, w_kv.shape[0]), BF16))(
        ids, w_stack, w_there
    )

    cosine, sine = tables(longest, seq_total, 128)
    out, gq, kv_term, kv_turned, x_all = call(
        lambda *refs: attention_kernel(longest, *refs),
        [smem] * 3 + [vmem] * 9,
        (vmem,) * 5,
        (
            shape((rows, 128), BF16),
            shape((rows, 128), BF16),
            shape((256, rows), BF16),
            shape((rows, 256), BF16),
            shape((32, rows, 128), BF16),
        ),
    )(
        ids, lengths, dest, x_mine, x_there, w_query, w_head, grad_att,
        cosine, sine, cosine.T.copy(), sine.T.copy(),
    )

    most, full = shape((8, 288, 128), BF16), shape((8, 256, 128), BF16)
    quad, slim, block = shape((4, 256, 128), BF16), shape((8, 32, 128), BF16), (rows, 128)
    mine, other = call(input_kernel, [smem] + [vmem] * 5, (vmem,) * 2, (most, most), 3)(
        ids, w_query, w_head, gq, kv_turned, kv_term
    )
    theirs = lax.ppermute(other, "c", SWAP)
    around = [[(i, (i + s) % 4) for i in range(4)] for s in range(4)]
    g0, g1, g3, low, high = call(
        weight_kernel, [smem] + [vmem] * 4, (vmem,) * 5, (full, full, full, quad, quad)
    )(ids, x_all, grad_out, out, gq)
    part = call(half_kernel, [vmem] * 2 + [anyw], vmem, most)(mine, theirs, g0)
    low, high, part = lax.optimization_barrier((low, high, part))
    part = lax.all_to_all(part, YY, 0, 0, tiled=True)
    low = lax.ppermute(low, "x", around[1])
    high = lax.ppermute(high, "x", around[3])
    h1, h3 = call(fold_kernel, [vmem] * 4, (vmem,) * 2, (full, full))(g1, g3, low, high)
    h1, h3 = lax.ppermute(h1, "x", around[1]), lax.ppermute(h3, "x", around[3])
    keep, send, *ks = call(
        collect_kernel, [smem] + [vmem] * 2, (vmem,) * 6, (shape(block, F32), shape(block, BF16)) + (slim,) * 4
    )(ids, part, x_all)
    ks = ks[:1] + [lax.ppermute(ks[s], "x", around[s]) for s in (1, 2, 3)]
    total, send = call(sum_kernel, [vmem] * 8, (vmem,) * 2, (most, shape(block, BF16)))(g0, h1, h3, *ks, send)
    grad_input = (keep + lax.ppermute(send, "zh", SWAP).astype(F32)).astype(BF16)

    total = lax.all_to_all(total.reshape(4, 576, 128), "za", 0, 0, tiled=True)
    total = jnp.sum(total.astype(F32), axis=0).reshape(2, 288, 128)
    send = jnp.where(own_zb == 0, total[1], total[0]).astype(BF16)
    query, wout, kv = call(
        last_kernel, [smem] + [vmem] * 2, (vmem,) * 3, (shape(block, F32), shape(block, F32), shape((32, 128), F32))
    )(ids, total, lax.ppermute(send, "zb", SWAP))
    return grad_input, query, kv.T, wout


def solution(mesh):
    fine = Mesh(mesh.devices.reshape(SIZES), AXES)
    placed = (P(DP, TP), P(DP, None), P(None, TP), P(None, TP), P(TP, None), P(), P())
    return jax.shard_map(
        body,
        mesh=fine,
        in_specs=placed,
        out_specs=(P(DP, TP), P(DP, TP), P(DP, TP), P(TP, DP)),
        check_vma=False,
    )
```

```python
import math

import jax
import jax.numpy as jnp
import numpy as np
from jax import lax
from jax.experimental import pallas as pl
from jax.experimental.pallas import tpu as pltpu
from jax.sharding import Mesh
from jax.sharding import PartitionSpec as P

AXES = ("x", "zb", "za", "zh", "yh", "yl", "c")
SIZES = (4, 2, 4, 2, 2, 4, 2)
DP = ("x", "zb", "za")
YY = ("yh", "yl")
TP = ("zh", "yh", "yl", "c")
PEERS = ("yl", "c")
F32 = jnp.float32
BF16 = jnp.bfloat16
SWAP = [(0, 1), (1, 0)]
G, OX, OC, OYL, OZH, OYH, OZB = 0, 1, 2, 3, 4, 5, 6


def dot(left, right, dims):
    return lax.dot_general(left, right, (dims, ((), ())), preferred_element_type=F32)


def tables(longest, seq_total, head_dim):
    frequency = np.exp(
        np.arange(head_dim // 2, dtype=np.float32) * np.float32(-2.0 * math.log(1000000.0) / head_dim)
    ).astype(np.float32)
    angles = (np.arange(longest, dtype=np.float32)[:, None] * frequency).astype(np.float32)
    cosine, sine = np.cos(angles), np.sin(angles)
    cosine = np.tile(np.concatenate([cosine, cosine], -1), (seq_total, 1)).astype(np.float32)
    signed = np.tile(np.concatenate([-sine, sine], -1), (seq_total, 1)).astype(np.float32)
    return cosine, signed


def aligned(index, size):
    return pl.ds(pl.multiple_of(index * size, size), size)


def incoming(ids_ref, dest_ref):
    seq_total, groups = dest_ref.shape
    senders = [lax.rem(ids_ref[G] + groups - dest_ref[j, 0], groups) for j in range(seq_total)]
    ranks = []
    for j in range(seq_total):
        rank = jnp.int32(0)
        for i in range(seq_total):
            rank = rank + (senders[i] < senders[j]).astype(jnp.int32)
        ranks.append(rank)
    return senders, ranks


def outgoing_kernel(ids_ref, len_any, dest_any, x_any, out_ref, len_ref, dest_ref, x_ref, sem):
    copies = [
        pltpu.make_async_copy(source, target, sem.at[n])
        for n, (source, target) in enumerate(((len_any, len_ref), (dest_any, dest_ref), (x_any, x_ref)))
    ]
    for copy in copies:
        copy.start()
    seq_total, groups = dest_ref.shape
    longest = out_ref.shape[1]
    tokens = x_ref.shape[0]
    group = ids_ref[G]
    out_ref[...] = jnp.zeros_like(out_ref)
    place = lax.broadcasted_iota(jnp.int32, (longest, tokens), 0)
    token = lax.broadcasted_iota(jnp.int32, (longest, tokens), 1)
    for copy in copies:
        copy.wait()
    start = jnp.int32(0)
    for j in range(seq_total):
        size = len_ref[j, group]
        chosen = jnp.where((token == place + start) & (place < size), 1.0, 0.0).astype(BF16)
        to = lax.rem(group + dest_ref[j, 0], groups)
        out_ref[to] = dot(chosen, x_ref[...], ((1,), (0,))).astype(BF16)
        start = start + size


def incoming_kernel(ids_ref, dest_ref, x_ref, *refs):
    out_ref = refs[-1]
    longest = x_ref.shape[1]
    senders, ranks = incoming(ids_ref, dest_ref)
    for sender, rank in zip(senders, ranks):
        out_ref[aligned(rank, longest), :] = x_ref[sender]


def spread_kernel(ids_ref, own_ref, other_ref, *refs):
    out_ref = refs[-1]
    zh = ids_ref[OZH]
    for i in range(out_ref.shape[0]):
        out_ref[i, zh] = own_ref[...]
        out_ref[i, 1 - zh] = other_ref[...]


def stack_kernel(*refs):
    out_ref = refs[-1]
    for rel in range(4):
        out_ref[rel] = refs[rel][...]


def head_kernel(ids_ref, here_ref, there_ref, out_ref):
    for rel in range(4):
        for flip, source in enumerate((here_ref, there_ref)):
            peer = (ids_ref[OYL] ^ rel) * 2 + (ids_ref[OC] ^ flip)
            out_ref[aligned(peer, 32), :] = source[rel]


def attention_kernel(longest, ids_ref, len_ref, dest_ref, xm_ref, xt_ref, wq_ref, wh_ref, ga_ref,
                     cos_ref, sin_ref, cost_ref, sint_ref, o_ref, gq_ref, kvg_ref, gap_ref, x_ref):
    rows, hd = ga_ref.shape
    inv_scale = 1.0 / math.sqrt(hd)

    def turn(v):
        return jnp.concatenate([v[:, hd // 2:], v[:, : hd // 2]], 1)

    def turn_t(v):
        return jnp.concatenate([v[hd // 2:], v[: hd // 2]], 0)

    q = jnp.zeros((rows, hd), F32)
    kv = jnp.zeros((2 * hd, rows), F32)
    for part_ref, core in ((xm_ref, ids_ref[OC]), (xt_ref, 1 - ids_ref[OC])):
        for y in range(8):
            for zh in range(2):
                block = zh * 16 + y * 2 + core
                cut = aligned(block, 128)
                xb = part_ref[y, zh]
                x_ref[block] = xb
                q = q + dot(xb, wq_ref[cut, :], ((1,), (0,)))
                kv = kv + dot(wh_ref[:, cut], xb, ((1,), (1,)))
    cosine, sine, cosine_t, sine_t = cos_ref[...], sin_ref[...], cost_ref[...], sint_ref[...]
    q = q.astype(BF16).astype(F32)
    q = (q * cosine + turn(q) * sine).astype(BF16)
    kv = kv.astype(BF16)
    k = kv[:hd].astype(F32)
    k = (k * cosine_t + turn_t(k) * sine_t).astype(BF16)
    v = kv[hd:]
    ga = ga_ref[...]
    qi = lax.broadcasted_iota(jnp.int32, (rows, rows), 0)
    ki = lax.broadcasted_iota(jnp.int32, (rows, rows), 1)
    ends = jnp.zeros((rows, rows), jnp.int32)
    starts = jnp.zeros((rows, rows), jnp.int32)
    senders, ranks = incoming(ids_ref, dest_ref)
    for j in range(rows // longest):
        first = ranks[j] * longest
        here = (qi >= first) & (qi < first + longest)
        starts = jnp.where(here, first, starts)
        ends = jnp.where(here, first + len_ref[j, senders[j]], ends)
    allowed = (ki >= starts) & (ki <= qi) & (ki < ends)
    scores = jnp.where(allowed, dot(q, k, ((1,), (0,))) * inv_scale, -1e30)
    highest = jnp.max(scores, axis=1, keepdims=True)
    weights = jnp.where(allowed, jnp.exp(scores - highest), 0.0)
    probs = weights / jnp.sum(weights, axis=1, keepdims=True)
    probs = jnp.where(qi < ends, probs, 0.0)
    low = probs.astype(BF16)
    o_ref[...] = dot(low, v, ((1,), (1,))).astype(BF16)
    gp = dot(ga, v, ((1,), (0,)))
    centre = jnp.sum(probs * gp, axis=1, keepdims=True)
    gs = (probs * (gp - centre) * inv_scale).astype(BF16)
    gq = dot(gs, k, ((1,), (1,)))
    gq_ref[...] = (gq * cosine - turn(gq) * sine).astype(BF16)
    gk = dot(q, gs, ((0,), (0,)))
    gk = (gk * cosine_t - turn_t(gk) * sine_t).astype(BF16)
    gv = dot(ga, low, ((0,), (0,))).astype(BF16)
    kvg_ref[:hd, :] = gk
    kvg_ref[hd:, :] = gv
    gap_ref[:, :hd] = gk.astype(F32).T.astype(BF16)
    gap_ref[:, hd:] = gv.astype(F32).T.astype(BF16)


def input_kernel(ids_ref, wq_ref, wh_ref, gq_ref, kvt_ref, term_ref, mine_ref, other_ref):
    gq, kvt = gq_ref[...], kvt_ref[...]
    for out_ref, c in ((other_ref, 1 - ids_ref[OC]), (mine_ref, ids_ref[OC])):
        for y in range(8):
            for zh in range(2):
                cut = aligned(zh * 16 + y * 2 + c, 128)
                part = dot(gq, wq_ref[cut, :], ((1,), (1,))) + dot(kvt, wh_ref[:, cut], ((1,), (0,)))
                out_ref[y, zh * 128 : zh * 128 + 128, :] = part.astype(BF16)
            term = term_ref[aligned((y & 3) * 2 + c, 32), :]
            out_ref[y, 256:288, :] = jnp.where(ids_ref[OYH] == y >> 2, term, jnp.zeros_like(term))


def row_of(yl, c):
    return ((yl & 1) * 2 + c) * 2 + (yl >> 1)


def weight_kernel(ids_ref, x_ref, go_ref, o_ref, gq_ref, g0_ref, g1_ref, g3_ref, low_ref, high_ref):
    gq, out = gq_ref[...], o_ref[...]
    for s, refs in ((2, (low_ref, high_ref)), (1, (g1_ref,)), (3, (g3_ref,)), (0, (g0_ref,))):
        x = (ids_ref[OX] + s) & 3
        for yl in range(4):
            for c in range(2):
                row, block = row_of(yl, c), x * 8 + yl * 2 + c
                ref = refs[row // 4 if s == 2 else 0]
                row = row % 4 if s == 2 else row
                ref[row, 0:128, :] = dot(x_ref[block], gq, ((0,), (0,))).astype(BF16)
                ref[row, 128:256, :] = dot(out, go_ref[:, aligned(block, 128)], ((0,), (0,))).astype(BF16)


def half_kernel(mine_ref, theirs_ref, after_ref, out_ref):
    out_ref[...] = (mine_ref[...].astype(F32) + theirs_ref[...].astype(F32)).astype(BF16)


def collect_kernel(ids_ref, part_ref, x_ref, keep_ref, send_ref, *k_refs):
    total = jnp.sum(part_ref[...].astype(F32), axis=0)
    first = ids_ref[OZH] == 0
    keep_ref[...] = jnp.where(first, total[:128], total[128:256])
    send_ref[...] = jnp.where(first, total[128:256], total[:128]).astype(BF16)
    kvg = total[256:288].astype(BF16)
    for s in (1, 2, 3, 0):
        x = (ids_ref[OX] + s) & 3
        for yl in range(4):
            for c in range(2):
                k_refs[s][row_of(yl, c)] = dot(kvg, x_ref[x * 8 + yl * 2 + c], ((1,), (0,))).astype(BF16)


def fold_kernel(g1_ref, g3_ref, low_ref, high_ref, h1_ref, h3_ref, one_ref, three_ref, sem):
    loads = [
        pltpu.make_async_copy(g1_ref.at[0:4], one_ref, sem.at[0]),
        pltpu.make_async_copy(g3_ref.at[4:8], three_ref, sem.at[1]),
    ]
    rest = [
        pltpu.make_async_copy(g1_ref.at[4:8], h1_ref.at[4:8], sem.at[2]),
        pltpu.make_async_copy(g3_ref.at[0:4], h3_ref.at[0:4], sem.at[3]),
    ]
    for copy in loads + rest:
        copy.start()
    loads[0].wait()
    h1_ref[0:4] = (one_ref[...].astype(F32) + low_ref[...].astype(F32)).astype(BF16)
    loads[1].wait()
    h3_ref[4:8] = (three_ref[...].astype(F32) + high_ref[...].astype(F32)).astype(BF16)
    for copy in rest:
        copy.wait()


def sum_kernel(*refs):
    send_ref, out_ref, late_ref = refs[7:]
    out_ref[:, 0:256, :] = sum(ref[...].astype(F32) for ref in refs[:3]).astype(BF16)
    out_ref[:, 256:288, :] = sum(ref[...].astype(F32) for ref in refs[3:7]).astype(BF16)
    late_ref[...] = send_ref[...]


def last_kernel(ids_ref, total_ref, there_ref, query_ref, wout_ref, kv_ref):
    own = total_ref[ids_ref[OZB]] + there_ref[...].astype(F32)
    query_ref[...] = own[0:128]
    wout_ref[...] = own[128:256]
    kv_ref[...] = own[256:288]


def body(x_source, grad_out, w_query, w_kv, w_out, lengths, dest):
    groups, seq_total = dest.shape
    lengths, dest = lengths.T, dest.T
    rows = grad_out.shape[0]
    longest = rows // seq_total
    vmem = pl.BlockSpec(memory_space=pltpu.VMEM)
    smem = pl.BlockSpec(memory_space=pltpu.SMEM)
    anyw = pl.BlockSpec(memory_space=pl.ANY)
    shape = jax.ShapeDtypeStruct
    own_x, own_c, own_yl = lax.axis_index("x"), lax.axis_index("c"), lax.axis_index("yl")
    own_zh, own_zb = lax.axis_index("zh"), lax.axis_index("zb")
    ids = jnp.stack([lax.axis_index(DP), own_x, own_c, own_yl, own_zh, lax.axis_index("yh"), own_zb]).astype(jnp.int32)

    def call(kernel, ins, outs, out_shape, micros=1, scratch=(), mib=32):
        params = pltpu.CompilerParams(vmem_limit_bytes=mib * 1024 * 1024)
        cost = pl.CostEstimate(flops=micros * 10**9, bytes_accessed=micros * 3_600_000, transcendentals=0)
        return pl.pallas_call(
            kernel, out_shape=out_shape, in_specs=ins, out_specs=outs, compiler_params=params, cost_estimate=cost,
            scratch_shapes=scratch,
        )

    outgoing = call(
        outgoing_kernel, [smem] + [anyw] * 3, vmem, shape((groups, longest, 128), BF16),
        scratch=[
            pltpu.SMEM(lengths.shape, jnp.int32),
            pltpu.SMEM(dest.shape, jnp.int32),
            pltpu.VMEM(x_source.shape, BF16),
            pltpu.SemaphoreType.DMA((3,)),
        ],
        mib=60,
    )(ids, lengths, dest, x_source)
    received = lax.all_to_all(outgoing, DP, 0, 0, tiled=True)
    w_own = w_kv.T
    across = [[(i, i ^ s) for i in range(4)] for s in range(4)]
    w_parts = [w_own] + [lax.ppermute(w_own, "yl", across[s]) for s in (1, 2, 3)]
    grad_att = dot(grad_out, w_out, ((1,), (1,))).astype(BF16)

    half = shape((8, 2, rows, 128), BF16)
    x_slice = call(incoming_kernel, [smem] * 2 + [vmem, anyw, anyw], vmem, shape((rows, 128), BF16))(
        ids, dest, received, w_parts[1], grad_att
    )
    x_other = lax.ppermute(x_slice, "zh", SWAP)
    spread = call(spread_kernel, [smem] + [vmem] * 2 + [anyw] * 2, vmem, half)(ids, x_slice, x_other, *w_parts[2:])
    x_mine = lax.all_to_all(spread, YY, 0, 0, tiled=True)
    x_there = lax.ppermute(x_mine, "c", SWAP)
    w_stack = call(stack_kernel, [vmem] * 4 + [anyw], vmem, shape((4,) + w_own.shape, BF16))(*w_parts, spread)
    w_there = lax.ppermute(w_stack, "c", SWAP)
    w_head = call(head_kernel, [smem] + [vmem] * 2, vmem, shape((256, w_kv.shape[0]), BF16))(
        ids, w_stack, w_there
    )

    cosine, sine = tables(longest, seq_total, 128)
    out, gq, kv_term, kv_turned, x_all = call(
        lambda *refs: attention_kernel(longest, *refs),
        [smem] * 3 + [vmem] * 9,
        (vmem,) * 5,
        (
            shape((rows, 128), BF16),
            shape((rows, 128), BF16),
            shape((256, rows), BF16),
            shape((rows, 256), BF16),
            shape((32, rows, 128), BF16),
        ),
    )(
        ids, lengths, dest, x_mine, x_there, w_query, w_head, grad_att,
        cosine, sine, cosine.T.copy(), sine.T.copy(),
    )

    most, full = shape((8, 288, 128), BF16), shape((8, 256, 128), BF16)
    quad, slim, block = shape((4, 256, 128), BF16), shape((8, 32, 128), BF16), (rows, 128)
    mine, other = call(input_kernel, [smem] + [vmem] * 5, (vmem,) * 2, (most, most), 3)(
        ids, w_query, w_head, gq, kv_turned, kv_term
    )
    theirs = lax.ppermute(other, "c", SWAP)
    around = [[(i, (i + s) % 4) for i in range(4)] for s in range(4)]
    g0, g1, g3, low, high = call(
        weight_kernel, [smem] + [vmem] * 4, (vmem,) * 5, (full, full, full, quad, quad)
    )(ids, x_all, grad_out, out, gq)
    part = call(half_kernel, [vmem] * 2 + [anyw], vmem, most)(mine, theirs, g0)
    low, high, part = lax.optimization_barrier((low, high, part))
    part = lax.all_to_all(part, YY, 0, 0, tiled=True)
    low = lax.ppermute(low, "x", around[1])
    high = lax.ppermute(high, "x", around[3])
    h1, h3 = call(
        fold_kernel, [anyw] * 2 + [vmem] * 2, (vmem,) * 2, (full, full),
        scratch=[pltpu.VMEM((4, 256, 128), BF16)] * 2 + [pltpu.SemaphoreType.DMA((4,))],
        mib=60,
    )(g1, g3, low, high)
    h1, h3 = lax.ppermute(h1, "x", around[1]), lax.ppermute(h3, "x", around[3])
    keep, send, *ks = call(
        collect_kernel, [smem] + [vmem] * 2, (vmem,) * 6, (shape(block, F32), shape(block, BF16)) + (slim,) * 4
    )(ids, part, x_all)
    ks = ks[:1] + [lax.ppermute(ks[s], "x", around[s]) for s in (1, 2, 3)]
    total, send = call(sum_kernel, [vmem] * 8, (vmem,) * 2, (most, shape(block, BF16)))(g0, h1, h3, *ks, send)
    grad_input = (keep + lax.ppermute(send, "zh", SWAP).astype(F32)).astype(BF16)

    total = lax.all_to_all(total.reshape(4, 576, 128), "za", 0, 0, tiled=True)
    total = jnp.sum(total.astype(F32), axis=0).reshape(2, 288, 128)
    send = jnp.where(own_zb == 0, total[1], total[0]).astype(BF16)
    query, wout, kv = call(
        last_kernel, [smem] + [vmem] * 2, (vmem,) * 3, (shape(block, F32), shape(block, F32), shape((32, 128), F32))
    )(ids, total, lax.ppermute(send, "zb", SWAP))
    return grad_input, query, kv.T, wout


def solution(mesh):
    fine = Mesh(mesh.devices.reshape(SIZES), AXES)
    placed = (P(DP, TP), P(DP, None), P(None, TP), P(None, TP), P(TP, None), P(), P())
    return jax.shard_map(
        body,
        mesh=fine,
        in_specs=placed,
        out_specs=(P(DP, TP), P(DP, TP), P(DP, TP), P(TP, DP)),
        check_vma=False,
    )
```

```python
import math

import jax
import jax.numpy as jnp
import numpy as np
from jax import lax
from jax.experimental import pallas as pl
from jax.experimental.pallas import tpu as pltpu
from jax.sharding import Mesh
from jax.sharding import PartitionSpec as P

AXES = ("x", "zb", "za", "zh", "yh", "yl", "c")
SIZES = (4, 2, 4, 2, 2, 4, 2)
DP = ("x", "zb", "za")
YY = ("yh", "yl")
TP = ("zh", "yh", "yl", "c")
PEERS = ("yl", "c")
F32 = jnp.float32
BF16 = jnp.bfloat16
SWAP = [(0, 1), (1, 0)]
G, OX, OC, OYL, OZH, OYH, OZB = 0, 1, 2, 3, 4, 5, 6


def dot(left, right, dims):
    return lax.dot_general(left, right, (dims, ((), ())), preferred_element_type=F32)


def tables(longest, seq_total, head_dim):
    frequency = np.exp(
        np.arange(head_dim // 2, dtype=np.float32) * np.float32(-2.0 * math.log(1000000.0) / head_dim)
    ).astype(np.float32)
    angles = (np.arange(longest, dtype=np.float32)[:, None] * frequency).astype(np.float32)
    cosine, sine = np.cos(angles), np.sin(angles)
    cosine = np.tile(np.concatenate([cosine, cosine], -1), (seq_total, 1)).astype(np.float32)
    signed = np.tile(np.concatenate([-sine, sine], -1), (seq_total, 1)).astype(np.float32)
    return cosine, signed


def aligned(index, size):
    return pl.ds(pl.multiple_of(index * size, size), size)


def incoming(ids_ref, dest_ref):
    seq_total, groups = dest_ref.shape
    senders = [lax.rem(ids_ref[G] + groups - dest_ref[j, 0], groups) for j in range(seq_total)]
    ranks = []
    for j in range(seq_total):
        rank = jnp.int32(0)
        for i in range(seq_total):
            rank = rank + (senders[i] < senders[j]).astype(jnp.int32)
        ranks.append(rank)
    return senders, ranks


def outgoing_kernel(ids_ref, len_any, dest_any, x_any, out_ref, len_ref, dest_ref, x_ref, sem):
    copies = [
        pltpu.make_async_copy(source, target, sem.at[n])
        for n, (source, target) in enumerate(((len_any, len_ref), (dest_any, dest_ref), (x_any, x_ref)))
    ]
    for copy in copies:
        copy.start()
    seq_total, groups = dest_ref.shape
    longest = out_ref.shape[1]
    tokens = x_ref.shape[0]
    group = ids_ref[G]
    out_ref[...] = jnp.zeros_like(out_ref)
    place = lax.broadcasted_iota(jnp.int32, (longest, tokens), 0)
    token = lax.broadcasted_iota(jnp.int32, (longest, tokens), 1)
    for copy in copies:
        copy.wait()
    start = jnp.int32(0)
    for j in range(seq_total):
        size = len_ref[j, group]
        chosen = jnp.where((token == place + start) & (place < size), 1.0, 0.0).astype(BF16)
        to = lax.rem(group + dest_ref[j, 0], groups)
        out_ref[to] = dot(chosen, x_ref[...], ((1,), (0,))).astype(BF16)
        start = start + size


def incoming_kernel(ids_ref, dest_ref, x_ref, *refs):
    out_ref = refs[-1]
    longest = x_ref.shape[1]
    senders, ranks = incoming(ids_ref, dest_ref)
    for sender, rank in zip(senders, ranks):
        out_ref[aligned(rank, longest), :] = x_ref[sender]


def spread_kernel(ids_ref, own_ref, other_ref, *refs):
    out_ref = refs[-1]
    zh = ids_ref[OZH]
    for i in range(out_ref.shape[0]):
        out_ref[i, zh] = own_ref[...]
        out_ref[i, 1 - zh] = other_ref[...]


def stack_kernel(*refs):
    out_ref = refs[-1]
    for rel in range(4):
        out_ref[rel] = refs[rel][...]


def head_kernel(ids_ref, here_ref, there_ref, out_ref):
    for rel in range(4):
        for flip, source in enumerate((here_ref, there_ref)):
            peer = (ids_ref[OYL] ^ rel) * 2 + (ids_ref[OC] ^ flip)
            out_ref[aligned(peer, 32), :] = source[rel]


def attention_kernel(longest, ids_ref, len_ref, dest_ref, xm_ref, xt_ref, wq_ref, wh_ref, ga_ref,
                     cos_ref, sin_ref, cost_ref, sint_ref, o_ref, gq_ref, kvg_ref, gap_ref, x_ref):
    rows, hd = ga_ref.shape
    inv_scale = 1.0 / math.sqrt(hd)

    def turn(v):
        return jnp.concatenate([v[:, hd // 2:], v[:, : hd // 2]], 1)

    def turn_t(v):
        return jnp.concatenate([v[hd // 2:], v[: hd // 2]], 0)

    q = jnp.zeros((rows, hd), F32)
    kv = jnp.zeros((2 * hd, rows), F32)
    for part_ref, core in ((xm_ref, ids_ref[OC]), (xt_ref, 1 - ids_ref[OC])):
        for y in range(8):
            for zh in range(2):
                block = zh * 16 + y * 2 + core
                cut = aligned(block, 128)
                xb = part_ref[y, zh]
                x_ref[block] = xb
                q = q + dot(xb, wq_ref[cut, :], ((1,), (0,)))
                kv = kv + dot(wh_ref[:, cut], xb, ((1,), (1,)))
    cosine, sine, cosine_t, sine_t = cos_ref[...], sin_ref[...], cost_ref[...], sint_ref[...]
    q = q.astype(BF16).astype(F32)
    q = (q * cosine + turn(q) * sine).astype(BF16)
    kv = kv.astype(BF16)
    k = kv[:hd].astype(F32)
    k = (k * cosine_t + turn_t(k) * sine_t).astype(BF16)
    v = kv[hd:]
    ga = ga_ref[...]
    qi = lax.broadcasted_iota(jnp.int32, (rows, rows), 0)
    ki = lax.broadcasted_iota(jnp.int32, (rows, rows), 1)
    ends = jnp.zeros((rows, rows), jnp.int32)
    starts = jnp.zeros((rows, rows), jnp.int32)
    senders, ranks = incoming(ids_ref, dest_ref)
    for j in range(rows // longest):
        first = ranks[j] * longest
        here = (qi >= first) & (qi < first + longest)
        starts = jnp.where(here, first, starts)
        ends = jnp.where(here, first + len_ref[j, senders[j]], ends)
    allowed = (ki >= starts) & (ki <= qi) & (ki < ends)
    scores = jnp.where(allowed, dot(q, k, ((1,), (0,))) * inv_scale, -1e30)
    highest = jnp.max(scores, axis=1, keepdims=True)
    weights = jnp.where(allowed, jnp.exp(scores - highest), 0.0)
    probs = weights / jnp.sum(weights, axis=1, keepdims=True)
    probs = jnp.where(qi < ends, probs, 0.0)
    low = probs.astype(BF16)
    o_ref[...] = dot(low, v, ((1,), (1,))).astype(BF16)
    gp = dot(ga, v, ((1,), (0,)))
    centre = jnp.sum(probs * gp, axis=1, keepdims=True)
    gs = (probs * (gp - centre) * inv_scale).astype(BF16)
    gq = dot(gs, k, ((1,), (1,)))
    gq_ref[...] = (gq * cosine - turn(gq) * sine).astype(BF16)
    gk = dot(q, gs, ((0,), (0,)))
    gk = (gk * cosine_t - turn_t(gk) * sine_t).astype(BF16)
    gv = dot(ga, low, ((0,), (0,))).astype(BF16)
    kvg_ref[:hd, :] = gk
    kvg_ref[hd:, :] = gv
    gap_ref[:, :hd] = gk.astype(F32).T.astype(BF16)
    gap_ref[:, hd:] = gv.astype(F32).T.astype(BF16)


def input_kernel(ids_ref, wq_ref, wh_ref, gq_ref, kvt_ref, term_ref, mine_ref, other_ref):
    gq, kvt = gq_ref[...], kvt_ref[...]
    for out_ref, c in ((other_ref, 1 - ids_ref[OC]), (mine_ref, ids_ref[OC])):
        for y in range(8):
            for zh in range(2):
                cut = aligned(zh * 16 + y * 2 + c, 128)
                part = dot(gq, wq_ref[cut, :], ((1,), (1,))) + dot(kvt, wh_ref[:, cut], ((1,), (0,)))
                out_ref[y, zh * 128 : zh * 128 + 128, :] = part.astype(BF16)
            term = term_ref[aligned((y & 3) * 2 + c, 32), :]
            out_ref[y, 256:288, :] = jnp.where(ids_ref[OYH] == y >> 2, term, jnp.zeros_like(term))


def row_of(yl, c):
    return ((yl & 1) * 2 + c) * 2 + (yl >> 1)


def weight_kernel(ids_ref, x_ref, go_ref, o_ref, gq_ref, g0_ref, plus_ref, minus_ref, one_ref, three_ref):
    gq, out = gq_ref[...], o_ref[...]
    places = (
        lambda row: (g0_ref, row),
        lambda row: (plus_ref, row) if row >= 4 else (one_ref, row),
        lambda row: (minus_ref, row) if row >= 4 else (plus_ref, row),
        lambda row: (three_ref, row - 4) if row >= 4 else (minus_ref, row),
    )
    for s in (2, 1, 3, 0):
        x = (ids_ref[OX] + s) & 3
        for yl in range(4):
            for c in range(2):
                ref, row = places[s](row_of(yl, c))
                block = x * 8 + yl * 2 + c
                ref[row, 0:128, :] = dot(x_ref[block], gq, ((0,), (0,))).astype(BF16)
                ref[row, 128:256, :] = dot(out, go_ref[:, aligned(block, 128)], ((0,), (0,))).astype(BF16)


def half_kernel(mine_ref, theirs_ref, after_ref, out_ref):
    out_ref[...] = (mine_ref[...].astype(F32) + theirs_ref[...].astype(F32)).astype(BF16)


def collect_kernel(ids_ref, part_ref, x_ref, keep_ref, send_ref, *k_refs):
    total = jnp.sum(part_ref[...].astype(F32), axis=0)
    first = ids_ref[OZH] == 0
    keep_ref[...] = jnp.where(first, total[:128], total[128:256])
    send_ref[...] = jnp.where(first, total[128:256], total[:128]).astype(BF16)
    kvg = total[256:288].astype(BF16)
    for s in (1, 2, 3, 0):
        x = (ids_ref[OX] + s) & 3
        for yl in range(4):
            for c in range(2):
                k_refs[s][row_of(yl, c)] = dot(kvg, x_ref[x * 8 + yl * 2 + c], ((1,), (0,))).astype(BF16)


def fold_kernel(one_ref, three_ref, plus_ref, minus_ref, k1_ref, k3_ref, h1_ref, h3_ref):
    h1_ref[0:4] = (one_ref[...].astype(F32) + plus_ref[0:4].astype(F32)).astype(BF16)
    h3_ref[0:4] = (three_ref[...].astype(F32) + minus_ref[4:8].astype(F32)).astype(BF16)
    for row in range(8):
        h1_ref[4, row * 32 : row * 32 + 32, :] = k1_ref[row]
        h3_ref[4, row * 32 : row * 32 + 32, :] = k3_ref[row]


def sum_kernel(g0_ref, plus_ref, minus_ref, h1_ref, h3_ref, k0_ref, k2_ref, send_ref, out_ref, late_ref):
    out_ref[0:4, 0:256, :] = sum(v.astype(F32) for v in (g0_ref[0:4], minus_ref[0:4], h1_ref[0:4])).astype(BF16)
    out_ref[4:8, 0:256, :] = sum(v.astype(F32) for v in (g0_ref[4:8], plus_ref[4:8], h3_ref[0:4])).astype(BF16)
    for row in range(8):
        rows = slice(row * 32, row * 32 + 32)
        parts = (k0_ref[row], k2_ref[row], h1_ref[4, rows, :], h3_ref[4, rows, :])
        out_ref[row, 256:288, :] = sum(v.astype(F32) for v in parts).astype(BF16)
    late_ref[...] = send_ref[...]


def last_kernel(ids_ref, total_ref, there_ref, query_ref, wout_ref, kv_ref):
    own = total_ref[ids_ref[OZB]] + there_ref[...].astype(F32)
    query_ref[...] = own[0:128]
    wout_ref[...] = own[128:256]
    kv_ref[...] = own[256:288]


def body(x_source, grad_out, w_query, w_kv, w_out, lengths, dest):
    groups, seq_total = dest.shape
    lengths, dest = lengths.T, dest.T
    rows = grad_out.shape[0]
    longest = rows // seq_total
    vmem = pl.BlockSpec(memory_space=pltpu.VMEM)
    smem = pl.BlockSpec(memory_space=pltpu.SMEM)
    anyw = pl.BlockSpec(memory_space=pl.ANY)
    shape = jax.ShapeDtypeStruct
    own_x, own_c, own_yl = lax.axis_index("x"), lax.axis_index("c"), lax.axis_index("yl")
    own_zh, own_zb = lax.axis_index("zh"), lax.axis_index("zb")
    ids = jnp.stack([lax.axis_index(DP), own_x, own_c, own_yl, own_zh, lax.axis_index("yh"), own_zb]).astype(jnp.int32)

    def call(kernel, ins, outs, out_shape, micros=1, scratch=(), mib=32):
        params = pltpu.CompilerParams(vmem_limit_bytes=mib * 1024 * 1024)
        cost = pl.CostEstimate(flops=micros * 10**9, bytes_accessed=micros * 3_600_000, transcendentals=0)
        return pl.pallas_call(
            kernel, out_shape=out_shape, in_specs=ins, out_specs=outs, compiler_params=params, cost_estimate=cost,
            scratch_shapes=scratch,
        )

    outgoing = call(
        outgoing_kernel, [smem] + [anyw] * 3, vmem, shape((groups, longest, 128), BF16),
        scratch=[
            pltpu.SMEM(lengths.shape, jnp.int32),
            pltpu.SMEM(dest.shape, jnp.int32),
            pltpu.VMEM(x_source.shape, BF16),
            pltpu.SemaphoreType.DMA((3,)),
        ],
        mib=60,
    )(ids, lengths, dest, x_source)
    received = lax.all_to_all(outgoing, DP, 0, 0, tiled=True)
    w_own = w_kv.T
    across = [[(i, i ^ s) for i in range(4)] for s in range(4)]
    w_parts = [w_own] + [lax.ppermute(w_own, "yl", across[s]) for s in (1, 2, 3)]
    grad_att = dot(grad_out, w_out, ((1,), (1,))).astype(BF16)

    half = shape((8, 2, rows, 128), BF16)
    x_slice = call(incoming_kernel, [smem] * 2 + [vmem, anyw, anyw], vmem, shape((rows, 128), BF16))(
        ids, dest, received, w_parts[1], grad_att
    )
    x_other = lax.ppermute(x_slice, "zh", SWAP)
    spread = call(spread_kernel, [smem] + [vmem] * 2 + [anyw] * 2, vmem, half)(ids, x_slice, x_other, *w_parts[2:])
    x_mine = lax.all_to_all(spread, YY, 0, 0, tiled=True)
    x_there = lax.ppermute(x_mine, "c", SWAP)
    w_stack = call(stack_kernel, [vmem] * 4 + [anyw], vmem, shape((4,) + w_own.shape, BF16))(*w_parts, spread)
    w_there = lax.ppermute(w_stack, "c", SWAP)
    w_head = call(head_kernel, [smem] + [vmem] * 2, vmem, shape((256, w_kv.shape[0]), BF16))(
        ids, w_stack, w_there
    )

    cosine, sine = tables(longest, seq_total, 128)
    out, gq, kv_term, kv_turned, x_all = call(
        lambda *refs: attention_kernel(longest, *refs),
        [smem] * 3 + [vmem] * 9,
        (vmem,) * 5,
        (
            shape((rows, 128), BF16),
            shape((rows, 128), BF16),
            shape((256, rows), BF16),
            shape((rows, 256), BF16),
            shape((32, rows, 128), BF16),
        ),
    )(
        ids, lengths, dest, x_mine, x_there, w_query, w_head, grad_att,
        cosine, sine, cosine.T.copy(), sine.T.copy(),
    )

    most, full = shape((8, 288, 128), BF16), shape((8, 256, 128), BF16)
    quad, slim, block = shape((4, 256, 128), BF16), shape((8, 32, 128), BF16), (rows, 128)
    mine, other = call(input_kernel, [smem] + [vmem] * 5, (vmem,) * 2, (most, most), 3)(
        ids, w_query, w_head, gq, kv_turned, kv_term
    )
    theirs = lax.ppermute(other, "c", SWAP)
    around = [[(i, (i + s) % 4) for i in range(4)] for s in range(4)]
    g0, plus, minus, one, three = call(
        weight_kernel, [smem] + [vmem] * 4, (vmem,) * 5, (full, full, full, quad, quad)
    )(ids, x_all, grad_out, out, gq)
    part = call(half_kernel, [vmem] * 2 + [anyw], vmem, most)(mine, theirs, g0)
    plus, minus, part = lax.optimization_barrier((plus, minus, part))
    part = lax.all_to_all(part, YY, 0, 0, tiled=True)
    plus, minus = lax.ppermute(plus, "x", around[1]), lax.ppermute(minus, "x", around[3])
    keep, send, k0, k1, k2, k3 = call(
        collect_kernel, [smem] + [vmem] * 2, (vmem,) * 6, (shape(block, F32), shape(block, BF16)) + (slim,) * 4
    )(ids, part, x_all)
    five = shape((5, 256, 128), BF16)
    h1, h3 = call(fold_kernel, [vmem] * 6, (vmem,) * 2, (five, five))(one, three, plus, minus, k1, k3)
    h1, h3 = lax.ppermute(h1, "x", around[1]), lax.ppermute(h3, "x", around[3])
    k2 = lax.ppermute(k2, "x", around[2])
    total, send = call(sum_kernel, [vmem] * 8, (vmem,) * 2, (most, shape(block, BF16)))(
        g0, plus, minus, h1, h3, k0, k2, send
    )
    grad_input = (keep + lax.ppermute(send, "zh", SWAP).astype(F32)).astype(BF16)

    total = lax.all_to_all(total.reshape(4, 576, 128), "za", 0, 0, tiled=True)
    total = jnp.sum(total.astype(F32), axis=0).reshape(2, 288, 128)
    send = jnp.where(own_zb == 0, total[1], total[0]).astype(BF16)
    query, wout, kv = call(
        last_kernel, [smem] + [vmem] * 2, (vmem,) * 3, (shape(block, F32), shape(block, F32), shape((32, 128), F32))
    )(ids, total, lax.ppermute(send, "zb", SWAP))
    return grad_input, query, kv.T, wout


def solution(mesh):
    fine = Mesh(mesh.devices.reshape(SIZES), AXES)
    placed = (P(DP, TP), P(DP, None), P(None, TP), P(None, TP), P(TP, None), P(), P())
    return jax.shard_map(
        body,
        mesh=fine,
        in_specs=placed,
        out_specs=(P(DP, TP), P(DP, TP), P(DP, TP), P(TP, DP)),
        check_vma=False,
    )
```
